512 devices in a mesh: member: 32 (over z_lo, y, core), space: 16 (over x, z_hi).
Axes of the slice: x: 4, y: 8, z: 8 (z_hi: 4, z_lo: 2; z = z_hi * 2 + z_lo), core: 2. Of those that a mesh axis runs over, the one named last changes fastest.
Arguments:
- participant_swirls: float32 [64, 512, 512], P('member', 'space'), may hold values from -6 to 6
- driving_source: float32 [512, 512], P('space'), may hold values from -12 to 12
- mixing: float32 [64, 64], replicated, may hold values from -0.75 to 0.75
- probes: int32 [32768], P('space'), may hold values from 0 to 16383
- observed: float32 [32768], P('space'), may hold values from -6 to 6
Outputs:
- analysis: float32 [64, 512, 512], P('member', 'space')
- spread: float32 [64, 64], replicated
- projection: float32 [64], replicated
The draws below stay inside these ranges and needn't reach their ends.
Inputs may be any that keep to these rules, and one draw needn't show every extreme that they name: `probes`: each index names a cell of its own block's 32 rows, row-major with 512 columns.
All inputs are finite; a program needn't handle non-finite values.
Results may differ from the reference program's by a relative error of at most 0.0003.
Values may be sent and summed in bfloat16 or wider, within the bound.
A program may use at most 64 MiB of HBM per device.

```python
import math
import jax
import jax.numpy as jnp
from jax import lax

N = 512
KEEP = 160
PROBE_DEV = 2048
MEMBERS = 64
ROWS = 32
PROBES = 32768


def touch_ends(entries, key, low, top_value):
    index_at = [jax.random.randint(jax.random.fold_in(key, axis), (), 0, length) for axis, length in enumerate(entries.shape)]
    main_axis = entries.shape.index(max(entries.shape))
    beside = index_at[:main_axis] + [(index_at[main_axis] + 1) % entries.shape[main_axis]] + index_at[main_axis + 1:]
    return entries.at[tuple(index_at)].set(low).at[tuple(beside)].set(top_value)


def levels(key, shape, split, low, high):
    gain, own = 1.0, jax.random.fold_in(key, 6)
    for axis_at, parts in split:
        steps = jnp.exp(jax.random.uniform(jax.random.fold_in(own, axis_at), (parts,), jnp.float32, low / len(split), high / len(split)))
        gain = gain * jnp.repeat(steps, shape[axis_at] // parts).reshape([-1 if axis == axis_at else 1 for axis in range(len(shape))])
    return gain


def centred(stream_key, shape, scale, bound, cuts=(), kind=jnp.bfloat16):
    level = levels(stream_key, shape, cuts, -0.22, 0.18) if cuts else 1.0
    drawn = jax.random.normal(stream_key, shape, jnp.float32) * scale * level
    return jnp.minimum(jnp.maximum(drawn, -bound), bound).astype(kind)


def setup_inputs(seed: int = 0) -> dict:
    splits = jax.random.split(jax.random.key(seed), 6)
    return {
        "participant_swirls": centred(splits[0], (MEMBERS, N, N), 1.0, 6.0, ((0, 32), (1, 16)), jnp.float32),
        "driving_source": centred(splits[1], (N, N), 2.0, 12.0, ((0, 16),), jnp.float32),
        "mixing": centred(splits[2], (MEMBERS, MEMBERS), MEMBERS ** -0.5, 0.75, (), jnp.float32),
        "probes": touch_ends(jax.random.randint(splits[3], (PROBES,), 0, ROWS * N), jax.random.fold_in(splits[3], 1), 0, (ROWS * N) - 1).astype(jnp.int32),
        "observed": centred(splits[4], (PROBES,), 1.0, 6.0, ((0, 16),), jnp.float32),
    }


DT_STEP = 0.1
VISCOSITY = 0.05

def wave_numbers():
    slots = jnp.arange(2 * KEEP, dtype=jnp.int32)
    along_x = jnp.where(slots < KEEP, slots, slots - 2 * KEEP)
    along_y = jnp.arange(KEEP, dtype=jnp.int32)
    scale = 2.0 * math.pi / N
    wave_x = (along_x.astype(jnp.float32) * scale)[:, None]
    wave_y = (along_y.astype(jnp.float32) * scale)[None, :]
    return (wave_x, wave_y)

def to_modes(field):
    spectrum = jnp.fft.rfft2(field) / (N * N)
    picked = jnp.concatenate([spectrum[:KEEP], spectrum[N - KEEP:]], 0)
    return picked[:, :KEEP]

def to_cells(modes):
    blank = jnp.zeros((N - 2 * KEEP, KEEP), modes.dtype)
    full = jnp.concatenate([modes[:KEEP], blank, modes[KEEP:]], 0)
    full = jnp.pad(full, ((0, 0), (0, N // 2 + 1 - KEEP)))
    return jnp.fft.irfft2(full, s=(N, N)) * (N * N)

def advance_model_once(curl_distribution, driving_source):
    wave_x, wave_y = wave_numbers()
    squared = wave_x * wave_x + wave_y * wave_y
    inverse_sq = jnp.where(squared > 0, 1.0 / jnp.where(squared > 0, squared, 1.0), 0.0)
    spectral = to_modes(curl_distribution)
    stream = spectral * inverse_sq
    vel_x = to_cells(1j * wave_y * stream)
    vel_y = to_cells(-1j * wave_x * stream)
    grad_x = to_cells(1j * wave_x * spectral)
    grad_y = to_cells(1j * wave_y * spectral)
    advect = vel_x * grad_x + vel_y * grad_y
    updated = spectral + DT_STEP * (-to_modes(advect) - VISCOSITY * squared * spectral)
    return to_cells(updated) + DT_STEP * driving_source

def reference(participant_swirls, driving_source, mixing, probes, observed):
    random_perturbations = lax.map(lambda lone_participant: advance_model_once(lone_participant, driving_source), participant_swirls)
    rounded = random_perturbations.astype(jnp.bfloat16)
    values = rounded.astype(jnp.float32)
    mean = lax.optimization_barrier(jnp.mean(values, 0))
    weights = lax.optimization_barrier(jnp.sum(mixing, 0))
    analysis = jnp.einsum('jm,jxy->mxy', mixing, values, precision=lax.Precision.HIGHEST)
    analysis = analysis + (1.0 - weights)[:, None, None] * mean[None]
    block = jnp.arange(PROBES, dtype=jnp.int32) // PROBE_DEV
    cells = block * (ROWS * N) + probes
    picked = values.reshape(MEMBERS, N * N)[:, cells]
    centre = lax.optimization_barrier(jnp.mean(picked, 0))
    anomaly = picked - centre[None]
    spread = jnp.dot(anomaly, anomaly.T, precision=lax.Precision.HIGHEST) / PROBES
    projection = jnp.dot(anomaly, observed - centre, precision=lax.Precision.HIGHEST) / math.sqrt(PROBES)
    return (analysis, spread, projection)
```

```python
import math

import jax
import jax.numpy as jnp
import ml_dtypes
import numpy as np
from jax import lax
from jax.experimental import pallas as pl
from jax.experimental.pallas import tpu as pltpu
from jax.sharding import PartitionSpec as P

N = 512
KEEP = 160
DT_STEP = 0.1
VISCOSITY = 0.05
MEMBERS = 64
ROWS = 32
PROBES = 32768
GM = 32
GS = 16
W = KEEP // GS
QP = 384
SWAP = False

F32 = jnp.float32
BF16 = jnp.bfloat16
MESH = pl.DeviceIdType.MESH
NN = (((1,), (0,)), ((), ()))
NT = (((1,), (1,)), ((), ()))


def halves(table):
    high = table.astype(np.float32).astype(ml_dtypes.bfloat16)
    low = (table - high.astype(np.float64)).astype(np.float32).astype(ml_dtypes.bfloat16)
    return [high, low]


def make_tables():
    cells = np.arange(N)
    slots = np.arange(2 * KEEP)
    kx = np.where(slots < KEEP, slots, slots - 2 * KEEP)
    ky = np.arange(KEEP)

    def trig(a, b):
        angle = (a[:, None] * b[None, :] % N) * (2.0 * np.pi / N)
        return np.cos(angle), np.sin(angle)

    cos_y, sin_y = trig(ky, cells)
    rows_f = np.concatenate([cos_y, -sin_y], 1)
    cos_x, sin_x = trig(cells, kx)
    cols_f = np.zeros((2 * N, QP))
    cols_f[:N, : 2 * KEEP] = cos_x / (N * N)
    cols_f[N:, : 2 * KEEP] = sin_x / (N * N)
    cols_g = np.zeros((2 * QP, N))
    cols_g[: 2 * KEEP] = cos_x.T
    cols_g[QP : QP + 2 * KEEP] = sin_x.T
    count = np.where(ky == 0, 1.0, 2.0)[:, None]
    rows_g4 = np.stack([cos_y * count, -sin_y * count], 0)
    rows_g4 = rows_g4.reshape(2, GS, W, N).transpose(1, 0, 2, 3).reshape(2 * KEEP, N).T
    out = []
    for t in (rows_f, cols_f, cols_g, rows_g4, cos_y * count, -sin_y * count):
        out += halves(np.ascontiguousarray(t))
    return out


TABLE_SHAPES = [(KEEP, 2 * N), (2 * N, QP), (2 * QP, N), (N, 2 * KEEP), (KEEP, N), (KEEP, N)]


def dot(a, b, dims=NN):
    return lax.dot_general(a, b, dims, preferred_element_type=F32)


def split(x):
    high = x.astype(BF16)
    return high, (x - high.astype(F32)).astype(BF16)


def swap(m, s):
    if not SWAP:
        return m, s
    z_lo, y, core = lax.div(m, 16), lax.rem(lax.div(m, 2), 8), lax.rem(m, 2)
    x, z_hi = lax.div(s, 4), lax.rem(s, 4)
    return lax.div(z_hi, 2) * 16 + y * 2 + lax.rem(z_hi, 2), x * 4 + z_lo * 2 + core


def lane_group(shape):
    return lax.div(lax.broadcasted_iota(jnp.int32, shape, len(shape) - 1), 32)


def pick_groups(pieces):
    group = lane_group(pieces[0].shape)
    low = jnp.where(group == 0, pieces[0], pieces[1])
    high = jnp.where(group == 2, pieces[2], pieces[3])
    return jnp.where(group < 2, low, high)


def turn(x, groups):
    groups %= 4
    return x if groups == 0 else pltpu.roll(x, 32 * groups, 1)


def gather_columns(recv):
    by_slot = [
        jnp.concatenate([recv[pl.ds(W * (4 * hi + slot), 16), :] for hi in range(4)], 0)
        for slot in range(4)
    ]
    rows = []
    for m in range(2):
        for c in range(2):
            t = c * 2 + m
            got = pick_groups([turn(by_slot[slot], slot - t) for slot in range(4)])
            rows.append(jnp.concatenate([got[16 * hi : 16 * hi + 16] for hi in range(4)], 1))
    return jnp.concatenate(rows, 0)


def times_i(w):
    return jnp.concatenate([-w[16:32], w[0:16], -w[48:64], w[32:48]], 0)


def to_slots(d, t_high, t_low):
    both = jnp.concatenate([d, -times_i(d)], 1)
    high, low = split(both)
    out = dot(jnp.concatenate([high, low], 0), t_high)
    return out[:64] + out[64:] + dot(high, t_low)


def to_cells(lhs, t_high, t_low):
    rows = lhs.shape[0]
    high, low = split(lhs)
    out = dot(jnp.concatenate([high, low], 0), t_high)
    return out[:rows] + out[rows:] + dot(high, t_low)


def stack_lanes(x):
    return jnp.concatenate([x[:, 128 * i : 128 * i + 128] for i in range(4)], 0)


def kernel(
    swirls, driving, mixing, probes, observed, *rest
):
    tables_hbm = rest[:12]
    analysis, spread, projection = rest[12:15]
    (
        f_v, drive_in, drive, mix_v, probes_v, obs_v,
        *more
    ) = rest[15:]
    tables = more[:12]
    (
        send1, recv1, send2, recv2, send3, recv3, send4, recv4, send5, recv5, send6, recv6,
        hist_s, hist_r, send_a, recv_a, send_b, recv_b, send_c, recv_c,
        spectrum, members_v, mixed_v,
        load_sem, table_sem, send_sem, recv_sem,
    ) = more[12:]
    m, s = lax.axis_index("member"), lax.axis_index("space")
    vm, vs = swap(m, s)

    def there(target):
        return dict(device_id={"member": target[0], "space": target[1]}, device_id_type=MESH)

    barrier = pltpu.get_barrier_semaphore()

    def hello(target):
        pl.semaphore_signal(barrier, inc=1, **there(target))

    greeted = (GS - 1) + (GM - 1)

    @pl.loop(1, GS)
    def _(d):
        hello(swap(vm, lax.rem(vs + d, GS)))

    @pl.loop(1, GM)
    def _(d):
        hello(swap(lax.rem(vm + d, GM), vs))

    if SWAP:
        @pl.loop(0, GS)
        def _(p):
            @pl.when(jnp.logical_or(vm != m, p != s))
            def _():
                hello((vm, p))

        @pl.loop(0, GM)
        def _(a):
            @pl.when(jnp.logical_or(vs != s, a != vm))
            def _():
                hello(swap(a, s))

        greeted = greeted + GS + GM - (vm == m).astype(jnp.int32) - (vs == s).astype(jnp.int32)

    loads = [
        pltpu.make_async_copy(src, dst, load_sem.at[i])
        for i, (src, dst) in enumerate(
            [(swirls, f_v), (driving, drive_in), (mixing, mix_v), (probes, probes_v), (observed, obs_v)]
        )
    ]
    table_loads = [
        pltpu.make_async_copy(src, dst, table_sem.at[i])
        for i, (src, dst) in enumerate(zip(tables_hbm, tables))
    ]
    loads[0].start()
    for copy in table_loads[:2]:
        copy.start()
    for copy in loads[1:]:
        copy.start()
    for copy in table_loads[2:]:
        copy.start()

    pending = []

    def copy_out(k, src, dst, target):
        return pltpu.make_async_remote_copy(
            src_ref=src, dst_ref=dst, send_sem=send_sem.at[k], recv_sem=recv_sem.at[k], **there(target)
        )

    def exchange(k, src, dst, axis, many=True):
        n = GS if axis == "space" else GM
        me = vs if axis == "space" else vm
        pltpu.make_async_copy(src(me), dst(me), recv_sem.at[k]).start()

        @pl.loop(1, n)
        def _(d):
            p = lax.rem(me + d, n)
            copy_out(k, src(p), dst(me), swap(vm, p) if axis == "space" else swap(p, vs)).start()

    def scatter(k, n, src, dst, target, is_self):
        @pl.loop(0, n)
        def _(p):
            mine = is_self(p)

            @pl.when(mine)
            def _():
                pltpu.make_async_copy(src(p), dst, recv_sem.at[k]).start()

            @pl.when(jnp.logical_not(mine))
            def _():
                copy_out(k, src(p), dst, target(p)).start()

    def finish(k, ref):
        pltpu.make_async_copy(ref, ref, recv_sem.at[k]).wait()

    def rows_of(ref, count):
        return lambda p: ref.at[pl.ds(count * p, count)]

    loads[0].wait()
    high, low = split(f_v[...])
    zero = jnp.zeros_like(high)

    def apart(x):
        return jnp.concatenate(
            [jnp.concatenate([x, zero], 1), jnp.concatenate([zero, x], 1)], 0
        )

    rhs_high = apart(high)
    table_loads[0].wait()
    table_loads[1].wait()
    out = dot(tables[0][...], jnp.concatenate([rhs_high, apart(low)], 0), NT)
    send1[...] = out[:, :128] + out[:, 128:] + dot(tables[1][...], rhs_high, NT)

    pl.semaphore_wait(barrier, greeted)
    if SWAP:
        scatter(
            0, GS, rows_of(send1, W), recv1.at[pl.ds(W * s, W)], lambda p: swap(m, p),
            lambda p: jnp.logical_and(vm == m, p == vs),
        )
    else:
        exchange(0, rows_of(send1, W), rows_of(recv1, W), "space")

    for copy in loads[1:]:
        copy.wait()
    if SWAP:
        @pl.when(jnp.logical_and(vm == m, vs == s))
        def _():
            pltpu.make_async_copy(drive_in, drive, recv_sem.at[10]).start()

        @pl.when(jnp.logical_or(vm != m, vs != s))
        def _():
            copy_out(10, drive_in, drive, (vm, vs)).start()
    tail = pl.ds(KEEP, 8)
    recv1[tail, :] = jnp.zeros((8, 128), F32)
    recv3[tail, :] = jnp.zeros((8, 128), F32)
    columns = lax.broadcasted_iota(jnp.int32, (N, 128), 0) + m * N

    def tally(i, total):
        cell = probes_v[pl.ds(i, 1), :]
        obs = obs_v[pl.ds(i, 1), :]
        a, rest_ = split(obs)
        left = obs - a.astype(F32)
        b = left.astype(BF16)
        c = (left - b.astype(F32)).astype(BF16)
        ones = jnp.ones((1, 128), BF16)
        lhs = jnp.concatenate([ones, a, b, c], 0)
        hit = jnp.where(columns == cell, 1.0, 0.0).astype(BF16)
        return total + dot(lhs, hit, NT)

    total = lax.fori_loop(0, 16, tally, jnp.zeros((4, N), F32))
    sums = total[1:2] + total[2:3] + total[3:4]
    for i in range(4):
        hist_s[i : i + 1, :] = total[0:1, 128 * i : 128 * i + 128]
        hist_s[4 + i : 5 + i, :] = sums[:, 128 * i : 128 * i + 128]
    if SWAP:
        @pl.when(jnp.logical_and(vm == m, vs == s))
        def _():
            pltpu.make_async_copy(hist_s, hist_r, recv_sem.at[11]).start()

        @pl.when(jnp.logical_or(vm != m, vs != s))
        def _():
            copy_out(11, hist_s, hist_r, (vm, vs)).start()
    weights = mix_v[...]
    weights = weights + (1.0 - jnp.sum(weights, 0, keepdims=True)) * (1.0 / MEMBERS)
    weights = weights.T
    w_high, w_rest = split(weights)
    w_left = weights - w_high.astype(F32)
    w_mid = w_left.astype(BF16)
    w_low = (w_left - w_mid.astype(F32)).astype(BF16)
    w_parts = jnp.concatenate([w_high, w_mid, w_low], 0)
    for copy in table_loads[2:]:
        copy.wait()

    scale = 2.0 * math.pi / N
    slot = lax.broadcasted_iota(jnp.int32, (16, QP), 1)
    slot = jnp.where(slot < KEEP, slot, jnp.where(slot < 2 * KEEP, slot - 2 * KEEP, 0))
    wave_x = slot.astype(F32) * scale
    wave_y = (lax.broadcasted_iota(jnp.int32, (16, QP), 0) + vs * W).astype(F32) * scale
    squared = wave_x * wave_x + wave_y * wave_y
    inverse = jnp.where(squared > 0, 1.0 / jnp.where(squared > 0, squared, 1.0), 0.0)

    def for_all(x):
        return jnp.concatenate([x] * 4, 0)

    finish(0, recv1.at[pl.ds(0, KEEP)])
    w = to_slots(gather_columns(recv1), tables[2][...], tables[3][...])
    spectrum[...] = w
    iw = times_i(w)
    pairs = [(wave_y * inverse, -wave_x * inverse), (wave_x, wave_y)]
    for h, pair in enumerate(pairs):
        lhs = jnp.concatenate(
            [jnp.concatenate([for_all(u) * iw, for_all(u) * -w], 1) for u in pair], 0
        )
        e = to_cells(lhs, tables[4][...], tables[5][...])
        parts = [stack_lanes(e[32 * g : 32 * g + 32]) for g in range(4)]
        for slot_ in range(4):
            got = pick_groups([turn(parts[g], g - slot_) for g in range(4)])
            for hi in range(4):
                for c in range(2):
                    send2[h, pl.ds(2 * W * (4 * hi + slot_) + W * c, W), :] = got[
                        32 * hi + 16 * c : 32 * hi + 16 * c + W
                    ]
        exchange(1 + h, rows_of(send2.at[h], 2 * W), rows_of(recv2.at[h], 2 * W), "space")

    def to_rows(h):
        high, low = split(recv2[h])
        out = dot(tables[6][...], jnp.concatenate([high, low], 1))
        return out[:, :128] + out[:, 128:] + dot(tables[7][...], high)

    finish(1, recv2.at[0])
    velocity = to_rows(0)
    finish(2, recv2.at[1])
    product = velocity * to_rows(1)
    product = product + pltpu.roll(product, 64, 1)
    first = lax.broadcasted_iota(jnp.int32, product.shape, 1) < 64
    rhs = jnp.concatenate([jnp.where(first, product, 0.0), jnp.where(first, 0.0, product)], 0)
    high, low = split(rhs)
    out = dot(tables[0][...], jnp.concatenate([high, low], 1))
    send3[...] = out[:, :128] + out[:, 128:] + dot(tables[1][...], high)
    exchange(3, rows_of(send3, W), rows_of(recv3, W), "space")

    finish(3, recv3.at[pl.ds(0, KEEP)])
    adv = to_slots(gather_columns(recv3), tables[2][...], tables[3][...])
    w = spectrum[...]
    new = w + DT_STEP * (-adv - VISCOSITY * for_all(squared) * w)
    e = to_cells(jnp.concatenate([new, times_i(new)], 1), tables[4][...], tables[5][...])
    parts = {
        c * 2 + k: stack_lanes(e[32 * k + 16 * c : 32 * k + 16 * c + 16])
        for k in range(2) for c in range(2)
    }
    for slot_ in range(4):
        got = pick_groups([turn(parts[g], g - slot_) for g in range(4)])
        for hi in range(4):
            send4[pl.ds(W * (4 * hi + slot_), W), :] = got[16 * hi : 16 * hi + W]
    exchange(4, rows_of(send4, W), rows_of(recv4, W), "space")

    if SWAP:
        finish(10, drive)
        finish(11, hist_r)
        drive_ref, hist = drive, hist_r
    else:
        drive_ref, hist = drive_in, hist_s
    forcing = DT_STEP * drive_ref[...]
    counts = jnp.concatenate([hist[i : i + 1, :] for i in range(4)], 1)
    obs_sums = jnp.concatenate([hist[4 + i : 5 + i, :] for i in range(4)], 1)

    finish(4, recv4)
    modes = recv4[...].T
    high, low = split(modes)
    out = dot(jnp.concatenate([high[:64], low[:64]], 0), tables[8][...])
    out = out + dot(jnp.concatenate([high[64:], low[64:]], 0), tables[10][...])
    fresh = out[:64] + out[64:] + dot(high[:64], tables[9][...]) + dot(high[64:], tables[11][...])
    fresh = fresh + jnp.concatenate([forcing, forcing], 0)
    rounded = fresh.astype(BF16).astype(F32)
    for k in range(2):
        for i in range(4):
            send5[:, 4 * k + i, :] = rounded[32 * k : 32 * k + 32, 128 * i : 128 * i + 128]
    exchange(5, lambda p: send5.at[p], lambda p: recv5.at[p], "member")

    finish(5, recv5)
    for k in range(2):
        for i in range(4):
            members_v[i, pl.ds(k, 32, stride=2), :] = recv5[:, 4 * k + i, :]
    values = jnp.concatenate([members_v[i] for i in range(4)], 1)

    centre = jnp.sum(values, 0, keepdims=True) * (1.0 / MEMBERS)
    anomaly = values - centre
    innovation = obs_sums - counts * centre
    other = jnp.concatenate(
        [anomaly * counts, innovation, jnp.zeros((63, N), F32)], 0
    )
    a_high, a_low = split(anomaly)
    b_high, b_low = split(other)
    send_a[...] = dot(a_high, b_high, NT) + dot(a_high, b_low, NT) + dot(a_low, b_high, NT)
    exchange(7, rows_of(send_a, 4), rows_of(recv_a, 4), "space")

    mixed = dot(w_parts, values.astype(BF16))
    mixed = mixed[:64] + mixed[64:128] + mixed[128:]
    for i in range(4):
        mixed_v[i] = mixed[:, 128 * i : 128 * i + 128]
    for k in range(2):
        for i in range(4):
            send6[:, 4 * k + i, :] = mixed_v[i, pl.ds(k, 32, stride=2), :]
    if SWAP:
        scatter(
            6, GM, lambda p: send6.at[p], recv6.at[vm], lambda p: (p, vs),
            lambda p: jnp.logical_and(vs == s, p == m),
        )
    else:
        exchange(6, lambda p: send6.at[p], lambda p: recv6.at[p], "member")

    finish(7, recv_a)
    chunk = recv_a[pl.ds(0, 4), :]
    for p in range(1, GS):
        chunk = chunk + recv_a[pl.ds(4 * p, 4), :]
    send_b[...] = chunk
    exchange(8, lambda p: send_b, rows_of(recv_b, 4), "member")

    finish(6, recv6)
    for k in range(2):
        for i in range(4):
            analysis[k, :, pl.ds(128 * i, 128)] = recv6[:, 4 * k + i, :]

    finish(8, recv_b)
    chunk = recv_b[pl.ds(0, 4), :]
    for p in range(1, GM):
        chunk = chunk + recv_b[pl.ds(4 * p, 4), :]
    send_c[...] = chunk
    exchange(9, lambda p: send_c, rows_of(recv_c, 4), "space")
    finish(9, recv_c)
    full = recv_c[...]
    spread[...] = full[:, :64] * (1.0 / PROBES)
    shape = (64, 64)
    diagonal = lax.broadcasted_iota(jnp.int32, shape, 0) == lax.broadcasted_iota(jnp.int32, shape, 1)
    column = jnp.where(diagonal, full[:, 64:65], 0.0)
    projection[...] = jnp.sum(column, 0, keepdims=True) * (1.0 / math.sqrt(PROBES))

    others = {
        0: send1.at[pl.ds(0, W * (GS - 1))],
        1: send2.at[0, pl.ds(0, 2 * W * (GS - 1))],
        2: send2.at[1, pl.ds(0, 2 * W * (GS - 1))],
        3: send3.at[pl.ds(0, W * (GS - 1))],
        4: send4.at[pl.ds(0, W * (GS - 1))],
        5: send5.at[pl.ds(0, GM - 1)],
        6: send6.at[pl.ds(0, GM - 1)],
        7: send_a.at[pl.ds(0, 4 * (GS - 1))],
        8: recv_b.at[pl.ds(0, 4 * (GM - 1))],
        9: recv_c.at[pl.ds(0, 4 * (GS - 1))],
    }

    def sent(k, ref):
        pltpu.make_async_copy(ref, ref, send_sem.at[k]).wait()

    for k, ref in others.items():
        sent(k, ref)
    if SWAP:
        @pl.when(vm != m)
        def _():
            sent(0, send1.at[pl.ds(0, W)])

        @pl.when(vs != s)
        def _():
            sent(6, send6.at[0])

        @pl.when(jnp.logical_or(vm != m, vs != s))
        def _():
            sent(10, drive_in)
            sent(11, hist_s)


def on_device(swirls, driving, mixing, probes, observed):
    tables = [jnp.asarray(t) for t in make_tables()]
    vmem = pltpu.VMEM
    lanes = 128
    buffers = [
        (64, N), (ROWS, N), (ROWS, N), (64, 64),
    ]
    scratch = [vmem(shape, F32) for shape in buffers]
    scratch += [vmem((16, 128), jnp.int32), vmem((16, 128), F32)]
    for shape in TABLE_SHAPES:
        scratch += [vmem(shape, BF16)] * 2
    for shape in [
        (KEEP, lanes), (KEEP + 8, lanes),
        (2, 2 * KEEP, lanes), (2, 2 * KEEP, lanes),
        (KEEP, lanes), (KEEP + 8, lanes),
        (KEEP, lanes), (KEEP, lanes),
        (GM, 8, lanes), (GM, 8, lanes), (GM, 8, lanes), (GM, 8, lanes),
        (8, lanes), (8, lanes),
        (64, lanes), (64, lanes), (4, lanes), (4 * GM, lanes), (4, lanes), (64, lanes),
        (64, QP), (4, 64, lanes), (4, 64, lanes),
    ]:
        scratch.append(vmem(shape, F32))
    dma = pltpu.SemaphoreType.DMA
    scratch += [dma((5,)), dma((12,)), dma((12,)), dma((12,))]
    anywhere = pl.BlockSpec(memory_space=pl.ANY)
    analysis, spread, projection = pl.pallas_call(
        kernel,
        out_shape=[
            jax.ShapeDtypeStruct((2, ROWS, N), F32),
            jax.ShapeDtypeStruct((64, 64), F32),
            jax.ShapeDtypeStruct((1, 64), F32),
        ],
        in_specs=[anywhere] * (5 + len(tables)),
        out_specs=[pl.BlockSpec(memory_space=pltpu.VMEM)] * 3,
        scratch_shapes=scratch,
        compiler_params=pltpu.CompilerParams(
            collective_id=0, has_side_effects=True, vmem_limit_bytes=48 * 2**20
        ),
    )(
        swirls.reshape(64, N), driving, mixing, probes.reshape(16, 128), observed.reshape(16, 128),
        *tables,
    )
    return analysis, spread, projection.reshape(64)


def solution(mesh):
    return jax.shard_map(
        on_device,
        mesh=mesh,
        in_specs=(P("member", "space", None), P("space", None), P(), P("space"), P("space")),
        out_specs=(P("member", "space", None), P(), P()),
        check_vma=False,
    )
```

```python
import math

import jax
import jax.numpy as jnp
import ml_dtypes
import numpy as np
from jax import lax
from jax.experimental import pallas as pl
from jax.experimental.pallas import tpu as pltpu
from jax.sharding import PartitionSpec as P

N = 512
KEEP = 160
DT_STEP = 0.1
VISCOSITY = 0.05
MEMBERS = 64
ROWS = 32
PROBES = 32768
GM = 32
GS = 16
W = KEEP // GS
QP = 384
SWAP = True

F32 = jnp.float32
BF16 = jnp.bfloat16
MESH = pl.DeviceIdType.MESH
NN = (((1,), (0,)), ((), ()))
NT = (((1,), (1,)), ((), ()))


def halves(table):
    high = table.astype(np.float32).astype(ml_dtypes.bfloat16)
    low = (table - high.astype(np.float64)).astype(np.float32).astype(ml_dtypes.bfloat16)
    return [high, low]


def make_tables():
    cells = np.arange(N)
    slots = np.arange(2 * KEEP)
    kx = np.where(slots < KEEP, slots, slots - 2 * KEEP)
    ky = np.arange(KEEP)

    def trig(a, b):
        angle = (a[:, None] * b[None, :] % N) * (2.0 * np.pi / N)
        return np.cos(angle), np.sin(angle)

    cos_y, sin_y = trig(ky, cells)
    rows_f = np.concatenate([cos_y, -sin_y], 1)
    cos_x, sin_x = trig(cells, kx)
    cols_f = np.zeros((2 * N, QP))
    cols_f[:N, : 2 * KEEP] = cos_x / (N * N)
    cols_f[N:, : 2 * KEEP] = sin_x / (N * N)
    cols_g = np.zeros((2 * QP, N))
    cols_g[: 2 * KEEP] = cos_x.T
    cols_g[QP : QP + 2 * KEEP] = sin_x.T
    count = np.where(ky == 0, 1.0, 2.0)[:, None]
    rows_g4 = np.stack([cos_y * count, -sin_y * count], 0)
    rows_g4 = rows_g4.reshape(2, GS, W, N).transpose(1, 0, 2, 3).reshape(2 * KEEP, N).T
    out = []
    for t in (rows_f, cols_f, cols_g, rows_g4, cos_y * count, -sin_y * count):
        out += halves(np.ascontiguousarray(t))
    return out


TABLE_SHAPES = [(KEEP, 2 * N), (2 * N, QP), (2 * QP, N), (N, 2 * KEEP), (KEEP, N), (KEEP, N)]


def dot(a, b, dims=NN):
    return lax.dot_general(a, b, dims, preferred_element_type=F32)


def split(x):
    high = x.astype(BF16)
    return high, (x - high.astype(F32)).astype(BF16)


def swap(m, s):
    if not SWAP:
        return m, s
    z_lo, y, core = lax.div(m, 16), lax.rem(lax.div(m, 2), 8), lax.rem(m, 2)
    x, z_hi = lax.div(s, 4), lax.rem(s, 4)
    return lax.div(z_hi, 2) * 16 + y * 2 + lax.rem(z_hi, 2), x * 4 + z_lo * 2 + core


def lane_group(shape):
    return lax.div(lax.broadcasted_iota(jnp.int32, shape, len(shape) - 1), 32)


def pick_groups(pieces):
    group = lane_group(pieces[0].shape)
    low = jnp.where(group == 0, pieces[0], pieces[1])
    high = jnp.where(group == 2, pieces[2], pieces[3])
    return jnp.where(group < 2, low, high)


def turn(x, groups):
    groups %= 4
    return x if groups == 0 else pltpu.roll(x, 32 * groups, 1)


def gather_columns(recv):
    by_slot = [
        jnp.concatenate([recv[pl.ds(W * (4 * hi + slot), 16), :] for hi in range(4)], 0)
        for slot in range(4)
    ]
    rows = []
    for m in range(2):
        for c in range(2):
            t = c * 2 + m
            got = pick_groups([turn(by_slot[slot], slot - t) for slot in range(4)])
            rows.append(jnp.concatenate([got[16 * hi : 16 * hi + 16] for hi in range(4)], 1))
    return jnp.concatenate(rows, 0)


def times_i(w):
    return jnp.concatenate([-w[16:32], w[0:16], -w[48:64], w[32:48]], 0)


def to_slots(d, t_high, t_low):
    both = jnp.concatenate([d, -times_i(d)], 1)
    high, low = split(both)
    out = dot(jnp.concatenate([high, low], 0), t_high)
    return out[:64] + out[64:] + dot(high, t_low)


def to_cells(lhs, t_high, t_low):
    rows = lhs.shape[0]
    high, low = split(lhs)
    out = dot(jnp.concatenate([high, low], 0), t_high)
    return out[:rows] + out[rows:] + dot(high, t_low)


def stack_lanes(x):
    return jnp.concatenate([x[:, 128 * i : 128 * i + 128] for i in range(4)], 0)


def kernel(
    swirls, driving, mixing, probes, observed, *rest
):
    tables_hbm = rest[:12]
    analysis, spread, projection = rest[12:15]
    (
        f_v, drive_in, drive, mix_v, probes_v, obs_v,
        *more
    ) = rest[15:]
    tables = more[:12]
    (
        send1, recv1, send2, recv2, send3, recv3, send4, recv4, send5, recv5, send6, recv6,
        hist_s, hist_r, send_a, recv_a, send_b, recv_b, send_c, recv_c,
        spectrum, members_v, mixed_v,
        load_sem, table_sem, send_sem, recv_sem,
    ) = more[12:]
    m, s = lax.axis_index("member"), lax.axis_index("space")
    vm, vs = swap(m, s)

    def there(target):
        return dict(device_id={"member": target[0], "space": target[1]}, device_id_type=MESH)

    barrier = pltpu.get_barrier_semaphore()

    def hello(target):
        pl.semaphore_signal(barrier, inc=1, **there(target))

    greeted = (GS - 1) + (GM - 1)

    @pl.loop(1, GS)
    def _(d):
        hello(swap(vm, lax.rem(vs + d, GS)))

    @pl.loop(1, GM)
    def _(d):
        hello(swap(lax.rem(vm + d, GM), vs))

    if SWAP:
        @pl.loop(0, GS)
        def _(p):
            @pl.when(jnp.logical_or(vm != m, p != s))
            def _():
                hello((vm, p))

        @pl.loop(0, GM)
        def _(a):
            @pl.when(jnp.logical_or(vs != s, a != vm))
            def _():
                hello(swap(a, s))

        greeted = greeted + GS + GM - (vm == m).astype(jnp.int32) - (vs == s).astype(jnp.int32)

    loads = [
        pltpu.make_async_copy(src, dst, load_sem.at[i])
        for i, (src, dst) in enumerate(
            [(swirls, f_v), (driving, drive_in), (mixing, mix_v), (probes, probes_v), (observed, obs_v)]
        )
    ]
    table_loads = [
        pltpu.make_async_copy(src, dst, table_sem.at[i])
        for i, (src, dst) in enumerate(zip(tables_hbm, tables))
    ]
    loads[0].start()
    for copy in table_loads[:2]:
        copy.start()
    for copy in loads[1:]:
        copy.start()
    for copy in table_loads[2:]:
        copy.start()

    pending = []

    def copy_out(k, src, dst, target):
        return pltpu.make_async_remote_copy(
            src_ref=src, dst_ref=dst, send_sem=send_sem.at[k], recv_sem=recv_sem.at[k], **there(target)
        )

    def exchange(k, src, dst, axis, many=True):
        n = GS if axis == "space" else GM
        me = vs if axis == "space" else vm
        pltpu.make_async_copy(src(me), dst(me), recv_sem.at[k]).start()

        @pl.loop(1, n)
        def _(d):
            p = lax.rem(me + d, n)
            copy_out(k, src(p), dst(me), swap(vm, p) if axis == "space" else swap(p, vs)).start()

    def scatter(k, n, src, dst, target, is_self):
        @pl.loop(0, n)
        def _(p):
            mine = is_self(p)

            @pl.when(mine)
            def _():
                pltpu.make_async_copy(src(p), dst, recv_sem.at[k]).start()

            @pl.when(jnp.logical_not(mine))
            def _():
                copy_out(k, src(p), dst, target(p)).start()

    def finish(k, ref):
        pltpu.make_async_copy(ref, ref, recv_sem.at[k]).wait()

    def rows_of(ref, count):
        return lambda p: ref.at[pl.ds(count * p, count)]

    loads[0].wait()
    high, low = split(f_v[...])
    zero = jnp.zeros_like(high)

    def apart(x):
        return jnp.concatenate(
            [jnp.concatenate([x, zero], 1), jnp.concatenate([zero, x], 1)], 0
        )

    rhs_high = apart(high)
    table_loads[0].wait()
    table_loads[1].wait()
    out = dot(tables[0][...], jnp.concatenate([rhs_high, apart(low)], 0), NT)
    send1[...] = out[:, :128] + out[:, 128:] + dot(tables[1][...], rhs_high, NT)

    pl.semaphore_wait(barrier, greeted)
    if SWAP:
        scatter(
            0, GS, rows_of(send1, W), recv1.at[pl.ds(W * s, W)], lambda p: swap(m, p),
            lambda p: jnp.logical_and(vm == m, p == vs),
        )
    else:
        exchange(0, rows_of(send1, W), rows_of(recv1, W), "space")

    for copy in loads[1:]:
        copy.wait()
    if SWAP:
        @pl.when(jnp.logical_and(vm == m, vs == s))
        def _():
            pltpu.make_async_copy(drive_in, drive, recv_sem.at[10]).start()

        @pl.when(jnp.logical_or(vm != m, vs != s))
        def _():
            copy_out(10, drive_in, drive, (vm, vs)).start()
    tail = pl.ds(KEEP, 8)
    recv1[tail, :] = jnp.zeros((8, 128), F32)
    recv3[tail, :] = jnp.zeros((8, 128), F32)
    columns = lax.broadcasted_iota(jnp.int32, (N, 128), 0) + m * N

    def tally(i, total):
        cell = probes_v[pl.ds(i, 1), :]
        obs = obs_v[pl.ds(i, 1), :]
        a, rest_ = split(obs)
        left = obs - a.astype(F32)
        b = left.astype(BF16)
        c = (left - b.astype(F32)).astype(BF16)
        ones = jnp.ones((1, 128), BF16)
        lhs = jnp.concatenate([ones, a, b, c], 0)
        hit = jnp.where(columns == cell, 1.0, 0.0).astype(BF16)
        return total + dot(lhs, hit, NT)

    total = lax.fori_loop(0, 16, tally, jnp.zeros((4, N), F32))
    sums = total[1:2] + total[2:3] + total[3:4]
    for i in range(4):
        hist_s[i : i + 1, :] = total[0:1, 128 * i : 128 * i + 128]
        hist_s[4 + i : 5 + i, :] = sums[:, 128 * i : 128 * i + 128]
    if SWAP:
        @pl.when(jnp.logical_and(vm == m, vs == s))
        def _():
            pltpu.make_async_copy(hist_s, hist_r, recv_sem.at[11]).start()

        @pl.when(jnp.logical_or(vm != m, vs != s))
        def _():
            copy_out(11, hist_s, hist_r, (vm, vs)).start()
    weights = mix_v[...]
    weights = weights + (1.0 - jnp.sum(weights, 0, keepdims=True)) * (1.0 / MEMBERS)
    weights = weights.T
    w_high, w_rest = split(weights)
    w_left = weights - w_high.astype(F32)
    w_mid = w_left.astype(BF16)
    w_low = (w_left - w_mid.astype(F32)).astype(BF16)
    w_parts = jnp.concatenate([w_high, w_mid, w_low], 0)
    for copy in table_loads[2:]:
        copy.wait()

    scale = 2.0 * math.pi / N
    slot = lax.broadcasted_iota(jnp.int32, (16, QP), 1)
    slot = jnp.where(slot < KEEP, slot, jnp.where(slot < 2 * KEEP, slot - 2 * KEEP, 0))
    wave_x = slot.astype(F32) * scale
    wave_y = (lax.broadcasted_iota(jnp.int32, (16, QP), 0) + vs * W).astype(F32) * scale
    squared = wave_x * wave_x + wave_y * wave_y
    inverse = jnp.where(squared > 0, 1.0 / jnp.where(squared > 0, squared, 1.0), 0.0)

    def for_all(x):
        return jnp.concatenate([x] * 4, 0)

    finish(0, recv1.at[pl.ds(0, KEEP)])
    w = to_slots(gather_columns(recv1), tables[2][...], tables[3][...])
    spectrum[...] = w
    iw = times_i(w)
    pairs = [(wave_y * inverse, -wave_x * inverse), (wave_x, wave_y)]
    for h, pair in enumerate(pairs):
        lhs = jnp.concatenate(
            [jnp.concatenate([for_all(u) * iw, for_all(u) * -w], 1) for u in pair], 0
        )
        e = to_cells(lhs, tables[4][...], tables[5][...])
        parts = [stack_lanes(e[32 * g : 32 * g + 32]) for g in range(4)]
        for slot_ in range(4):
            got = pick_groups([turn(parts[g], g - slot_) for g in range(4)])
            for hi in range(4):
                for c in range(2):
                    send2[h, pl.ds(2 * W * (4 * hi + slot_) + W * c, W), :] = got[
                        32 * hi + 16 * c : 32 * hi + 16 * c + W
                    ]
        exchange(1 + h, rows_of(send2.at[h], 2 * W), rows_of(recv2.at[h], 2 * W), "space")

    def to_rows(h):
        high, low = split(recv2[h])
        out = dot(tables[6][...], jnp.concatenate([high, low], 1))
        return out[:, :128] + out[:, 128:] + dot(tables[7][...], high)

    finish(1, recv2.at[0])
    velocity = to_rows(0)
    finish(2, recv2.at[1])
    product = velocity * to_rows(1)
    product = product + pltpu.roll(product, 64, 1)
    first = lax.broadcasted_iota(jnp.int32, product.shape, 1) < 64
    rhs = jnp.concatenate([jnp.where(first, product, 0.0), jnp.where(first, 0.0, product)], 0)
    high, low = split(rhs)
    out = dot(tables[0][...], jnp.concatenate([high, low], 1))
    send3[...] = out[:, :128] + out[:, 128:] + dot(tables[1][...], high)
    exchange(3, rows_of(send3, W), rows_of(recv3, W), "space")

    finish(3, recv3.at[pl.ds(0, KEEP)])
    adv = to_slots(gather_columns(recv3), tables[2][...], tables[3][...])
    w = spectrum[...]
    new = w + DT_STEP * (-adv - VISCOSITY * for_all(squared) * w)
    e = to_cells(jnp.concatenate([new, times_i(new)], 1), tables[4][...], tables[5][...])
    parts = {
        c * 2 + k: stack_lanes(e[32 * k + 16 * c : 32 * k + 16 * c + 16])
        for k in range(2) for c in range(2)
    }
    for slot_ in range(4):
        got = pick_groups([turn(parts[g], g - slot_) for g in range(4)])
        for hi in range(4):
            send4[pl.ds(W * (4 * hi + slot_), W), :] = got[16 * hi : 16 * hi + W]
    exchange(4, rows_of(send4, W), rows_of(recv4, W), "space")

    if SWAP:
        finish(10, drive)
        finish(11, hist_r)
        drive_ref, hist = drive, hist_r
    else:
        drive_ref, hist = drive_in, hist_s
    forcing = DT_STEP * drive_ref[...]
    counts = jnp.concatenate([hist[i : i + 1, :] for i in range(4)], 1)
    obs_sums = jnp.concatenate([hist[4 + i : 5 + i, :] for i in range(4)], 1)

    finish(4, recv4)
    modes = recv4[...].T
    high, low = split(modes)
    out = dot(jnp.concatenate([high[:64], low[:64]], 0), tables[8][...])
    out = out + dot(jnp.concatenate([high[64:], low[64:]], 0), tables[10][...])
    fresh = out[:64] + out[64:] + dot(high[:64], tables[9][...]) + dot(high[64:], tables[11][...])
    fresh = fresh + jnp.concatenate([forcing, forcing], 0)
    rounded = fresh.astype(BF16).astype(F32)
    for k in range(2):
        for i in range(4):
            send5[:, 4 * k + i, :] = rounded[32 * k : 32 * k + 32, 128 * i : 128 * i + 128]
    exchange(5, lambda p: send5.at[p], lambda p: recv5.at[p], "member")

    finish(5, recv5)
    for k in range(2):
        for i in range(4):
            members_v[i, pl.ds(k, 32, stride=2), :] = recv5[:, 4 * k + i, :]
    values = jnp.concatenate([members_v[i] for i in range(4)], 1)

    centre = jnp.sum(values, 0, keepdims=True) * (1.0 / MEMBERS)
    anomaly = values - centre
    innovation = obs_sums - counts * centre
    other = jnp.concatenate(
        [anomaly * counts, innovation, jnp.zeros((63, N), F32)], 0
    )
    a_high, a_low = split(anomaly)
    b_high, b_low = split(other)
    send_a[...] = dot(a_high, b_high, NT) + dot(a_high, b_low, NT) + dot(a_low, b_high, NT)
    exchange(7, rows_of(send_a, 4), rows_of(recv_a, 4), "space")

    mixed = dot(w_parts, values.astype(BF16))
    mixed = mixed[:64] + mixed[64:128] + mixed[128:]
    for i in range(4):
        mixed_v[i] = mixed[:, 128 * i : 128 * i + 128]
    for k in range(2):
        for i in range(4):
            send6[:, 4 * k + i, :] = mixed_v[i, pl.ds(k, 32, stride=2), :]
    if SWAP:
        scatter(
            6, GM, lambda p: send6.at[p], recv6.at[vm], lambda p: (p, vs),
            lambda p: jnp.logical_and(vs == s, p == m),
        )
    else:
        exchange(6, lambda p: send6.at[p], lambda p: recv6.at[p], "member")

    finish(7, recv_a)
    chunk = recv_a[pl.ds(0, 4), :]
    for p in range(1, GS):
        chunk = chunk + recv_a[pl.ds(4 * p, 4), :]
    send_b[...] = chunk
    exchange(8, lambda p: send_b, rows_of(recv_b, 4), "member")

    finish(6, recv6)
    for k in range(2):
        for i in range(4):
            analysis[k, :, pl.ds(128 * i, 128)] = recv6[:, 4 * k + i, :]

    finish(8, recv_b)
    chunk = recv_b[pl.ds(0, 4), :]
    for p in range(1, GM):
        chunk = chunk + recv_b[pl.ds(4 * p, 4), :]
    send_c[...] = chunk
    exchange(9, lambda p: send_c, rows_of(recv_c, 4), "space")
    finish(9, recv_c)
    full = recv_c[...]
    spread[...] = full[:, :64] * (1.0 / PROBES)
    shape = (64, 64)
    diagonal = lax.broadcasted_iota(jnp.int32, shape, 0) == lax.broadcasted_iota(jnp.int32, shape, 1)
    column = jnp.where(diagonal, full[:, 64:65], 0.0)
    projection[...] = jnp.sum(column, 0, keepdims=True) * (1.0 / math.sqrt(PROBES))

    others = {
        0: send1.at[pl.ds(0, W * (GS - 1))],
        1: send2.at[0, pl.ds(0, 2 * W * (GS - 1))],
        2: send2.at[1, pl.ds(0, 2 * W * (GS - 1))],
        3: send3.at[pl.ds(0, W * (GS - 1))],
        4: send4.at[pl.ds(0, W * (GS - 1))],
        5: send5.at[pl.ds(0, GM - 1)],
        6: send6.at[pl.ds(0, GM - 1)],
        7: send_a.at[pl.ds(0, 4 * (GS - 1))],
        8: recv_b.at[pl.ds(0, 4 * (GM - 1))],
        9: recv_c.at[pl.ds(0, 4 * (GS - 1))],
    }

    def sent(k, ref):
        pltpu.make_async_copy(ref, ref, send_sem.at[k]).wait()

    for k, ref in others.items():
        sent(k, ref)
    if SWAP:
        @pl.when(vm != m)
        def _():
            sent(0, send1.at[pl.ds(0, W)])

        @pl.when(vs != s)
        def _():
            sent(6, send6.at[0])

        @pl.when(jnp.logical_or(vm != m, vs != s))
        def _():
            sent(10, drive_in)
            sent(11, hist_s)


def on_device(swirls, driving, mixing, probes, observed):
    tables = [jnp.asarray(t) for t in make_tables()]
    vmem = pltpu.VMEM
    lanes = 128
    buffers = [
        (64, N), (ROWS, N), (ROWS, N), (64, 64),
    ]
    scratch = [vmem(shape, F32) for shape in buffers]
    scratch += [vmem((16, 128), jnp.int32), vmem((16, 128), F32)]
    for shape in TABLE_SHAPES:
        scratch += [vmem(shape, BF16)] * 2
    for shape in [
        (KEEP, lanes), (KEEP + 8, lanes),
        (2, 2 * KEEP, lanes), (2, 2 * KEEP, lanes),
        (KEEP, lanes), (KEEP + 8, lanes),
        (KEEP, lanes), (KEEP, lanes),
        (GM, 8, lanes), (GM, 8, lanes), (GM, 8, lanes), (GM, 8, lanes),
        (8, lanes), (8, lanes),
        (64, lanes), (64, lanes), (4, lanes), (4 * GM, lanes), (4, lanes), (64, lanes),
        (64, QP), (4, 64, lanes), (4, 64, lanes),
    ]:
        scratch.append(vmem(shape, F32))
    dma = pltpu.SemaphoreType.DMA
    scratch += [dma((5,)), dma((12,)), dma((12,)), dma((12,))]
    anywhere = pl.BlockSpec(memory_space=pl.ANY)
    analysis, spread, projection = pl.pallas_call(
        kernel,
        out_shape=[
            jax.ShapeDtypeStruct((2, ROWS, N), F32),
            jax.ShapeDtypeStruct((64, 64), F32),
            jax.ShapeDtypeStruct((1, 64), F32),
        ],
        in_specs=[anywhere] * (5 + len(tables)),
        out_specs=[pl.BlockSpec(memory_space=pltpu.VMEM)] * 3,
        scratch_shapes=scratch,
        compiler_params=pltpu.CompilerParams(
            collective_id=0, has_side_effects=True, vmem_limit_bytes=60 * 2**20
        ),
    )(
        swirls.reshape(64, N), driving, mixing, probes.reshape(16, 128), observed.reshape(16, 128),
        *tables,
    )
    return analysis, spread, projection.reshape(64)


def solution(mesh):
    return jax.shard_map(
        on_device,
        mesh=mesh,
        in_specs=(P("member", "space", None), P("space", None), P(), P("space"), P("space")),
        out_specs=(P("member", "space", None), P(), P()),
        check_vma=False,
    )
```

```python
import math

import jax
import jax.numpy as jnp
import ml_dtypes
import numpy as np
from jax import lax
from jax.experimental import pallas as pl
from jax.experimental.pallas import tpu as pltpu
from jax.sharding import PartitionSpec as P

N = 512
KEEP = 160
DT_STEP = 0.1
VISCOSITY = 0.05
MEMBERS = 64
ROWS = 32
PROBES = 32768
GM = 32
GS = 16
W = KEEP // GS
QP = 384

F32 = jnp.float32
BF16 = jnp.bfloat16
MESH = pl.DeviceIdType.MESH
NN = (((1,), (0,)), ((), ()))
NT = (((1,), (1,)), ((), ()))


def halves(table):
    high = table.astype(np.float32).astype(ml_dtypes.bfloat16)
    low = (table - high.astype(np.float64)).astype(np.float32).astype(ml_dtypes.bfloat16)
    return [high, low]


def make_tables():
    cells = np.arange(N)
    slots = np.arange(2 * KEEP)
    kx = np.where(slots < KEEP, slots, slots - 2 * KEEP)
    ky = np.arange(KEEP)

    def trig(a, b):
        angle = (a[:, None] * b[None, :] % N) * (2.0 * np.pi / N)
        return np.cos(angle), np.sin(angle)

    cos_y, sin_y = trig(ky, cells)
    rows_f = np.concatenate([cos_y, -sin_y], 1)
    cos_x, sin_x = trig(cells, kx)
    cols_f = np.zeros((2 * N, QP))
    cols_f[:N, : 2 * KEEP] = cos_x / (N * N)
    cols_f[N:, : 2 * KEEP] = sin_x / (N * N)
    cols_g = np.zeros((2 * QP, N))
    cols_g[: 2 * KEEP] = cos_x.T
    cols_g[QP : QP + 2 * KEEP] = sin_x.T
    count = np.where(ky == 0, 1.0, 2.0)[:, None]
    rows_g4 = np.stack([cos_y * count, -sin_y * count], 0)
    rows_g4 = rows_g4.reshape(2, GS, W, N).transpose(1, 0, 2, 3).reshape(2 * KEEP, N).T
    out = []
    for t in (rows_f, cols_f, cols_g, rows_g4, cos_y * count, -sin_y * count):
        out += halves(np.ascontiguousarray(t))
    return out


TABLE_SHAPES = [(KEEP, 2 * N), (2 * N, QP), (2 * QP, N), (N, 2 * KEEP), (KEEP, N), (KEEP, N)]


def dot(a, b, dims=NN):
    return lax.dot_general(a, b, dims, preferred_element_type=F32)


def split(x):
    high = x.astype(BF16)
    return high, (x - high.astype(F32)).astype(BF16)


def swap(m, s):
    z_lo, y, core = lax.div(m, 16), lax.rem(lax.div(m, 2), 8), lax.rem(m, 2)
    x, z_hi = lax.div(s, 4), lax.rem(s, 4)
    return lax.div(z_hi, 2) * 16 + y * 2 + lax.rem(z_hi, 2), x * 4 + z_lo * 2 + core


def far_first(k):
    return jnp.where(k == 0, 2, jnp.where(k == 3, 0, 2 * k - 1))


def far_first_of_eight(k):
    return jnp.where(lax.rem(k, 2) == 0, 4 + lax.div(k, 2), 4 - lax.div(k + 1, 2))


def space_peer(vs, i):
    x, z_lo, core = lax.div(vs, 4), lax.rem(lax.div(vs, 2), 2), lax.rem(vs, 2)
    k, near = lax.div(i, 4), lax.rem(i, 4)
    x = lax.rem(x + far_first(k), 4)
    z_lo = lax.rem(z_lo + 1 - lax.div(near, 2), 2)
    core = lax.rem(core + 1 - lax.rem(near, 2), 2)
    return x * 4 + z_lo * 2 + core


def member_peer(vm, i):
    z_hi, y = lax.div(vm, 16) * 2 + lax.rem(vm, 2), lax.rem(lax.div(vm, 2), 8)
    y = lax.rem(y + far_first_of_eight(lax.div(i, 4)), 8)
    z_hi = lax.rem(z_hi + far_first(lax.rem(i, 4)), 4)
    return lax.div(z_hi, 2) * 16 + y * 2 + lax.rem(z_hi, 2)


def lane_group(shape):
    return lax.div(lax.broadcasted_iota(jnp.int32, shape, len(shape) - 1), 32)


def pick_groups(pieces):
    group = lane_group(pieces[0].shape)
    low = jnp.where(group == 0, pieces[0], pieces[1])
    high = jnp.where(group == 2, pieces[2], pieces[3])
    return jnp.where(group < 2, low, high)


def turn(x, groups):
    groups %= 4
    return x if groups == 0 else pltpu.roll(x, 32 * groups, 1)


def gather_columns(recv):
    by_slot = [
        jnp.concatenate([recv[pl.ds(W * (4 * hi + slot), 16), :] for hi in range(4)], 0)
        for slot in range(4)
    ]
    rows = []
    for m in range(2):
        for c in range(2):
            t = c * 2 + m
            got = pick_groups([turn(by_slot[slot], slot - t) for slot in range(4)])
            rows.append(jnp.concatenate([got[16 * hi : 16 * hi + 16] for hi in range(4)], 1))
    return jnp.concatenate(rows, 0)


def times_i(w):
    return jnp.concatenate([-w[16:32], w[0:16], -w[48:64], w[32:48]], 0)


def to_slots(d, t_high, t_low):
    both = jnp.concatenate([d, -times_i(d)], 1)
    high, low = split(both)
    out = dot(jnp.concatenate([high, low], 0), t_high)
    return out[:64] + out[64:] + dot(high, t_low)


def to_cells(lhs, t_high, t_low):
    rows = lhs.shape[0]
    high, low = split(lhs)
    out = dot(jnp.concatenate([high, low], 0), t_high)
    return out[:rows] + out[rows:] + dot(high, t_low)


def stack_lanes(x):
    return jnp.concatenate([x[:, 128 * i : 128 * i + 128] for i in range(4)], 0)


def kernel(
    swirls, driving, mixing, probes, observed, *rest
):
    tables_hbm = rest[:12]
    rows_out, sums_out = rest[12:14]
    (
        f_v, drive_in, drive, mix_v, probes_v, obs_v,
        *more
    ) = rest[14:]
    tables = more[:12]
    (
        send1, recv1, send2, recv2, send3, recv3, send4, recv4, send5, recv5, send6, recv6,
        hist_s, hist_r, send_a, recv_a, send_b, recv_b, send_c, recv_c,
        spectrum, members_v, mixed_v, by_row, by_member,
        load_sem, table_sem, send_sem, recv_sem,
    ) = more[12:]
    m, s = lax.axis_index("member"), lax.axis_index("space")
    vm, vs = swap(m, s)

    def there(target):
        return dict(device_id={"member": target[0], "space": target[1]}, device_id_type=MESH)

    barrier = pltpu.get_barrier_semaphore()

    def hello(target):
        pl.semaphore_signal(barrier, inc=1, **there(target))

    @pl.loop(0, GS)
    def _(p):
        @pl.when(jnp.logical_or(vm != m, p != s))
        def _():
            hello((vm, p))

    @pl.loop(0, GS - 1)
    def _(i):
        hello(swap(vm, space_peer(vs, i)))

    @pl.loop(0, GM - 1)
    def _(i):
        hello(swap(member_peer(vm, i), vs))

    @pl.loop(0, GM)
    def _(a):
        @pl.when(jnp.logical_or(vs != s, a != vm))
        def _():
            hello(swap(a, s))

    greeted = 2 * (GS + GM - 1) - (vm == m).astype(jnp.int32) - (vs == s).astype(jnp.int32)

    loads = [
        pltpu.make_async_copy(src, dst, load_sem.at[i])
        for i, (src, dst) in enumerate(
            [(swirls, f_v), (driving, drive_in), (mixing, mix_v), (probes, probes_v), (observed, obs_v)]
        )
    ]
    table_loads = [
        pltpu.make_async_copy(src, dst, table_sem.at[i])
        for i, (src, dst) in enumerate(zip(tables_hbm, tables))
    ]
    loads[0].start()
    for copy in table_loads[:2]:
        copy.start()
    for copy in loads[1:]:
        copy.start()
    for copy in table_loads[2:]:
        copy.start()

    def copy_out(k, src, dst, target):
        return pltpu.make_async_remote_copy(
            src_ref=src, dst_ref=dst, send_sem=send_sem.at[k], recv_sem=recv_sem.at[k], **there(target)
        )

    def exchange(k, src, dst, axis):
        space = axis == "space"
        me = vs if space else vm

        @pl.loop(0, (GS if space else GM) - 1)
        def _(i):
            p = space_peer(vs, i) if space else member_peer(vm, i)
            copy_out(k, src(p), dst(me), swap(vm, p) if space else swap(p, vs)).start()

        pltpu.make_async_copy(src(me), dst(me), recv_sem.at[k]).start()

    def scatter(k, n, order, src, dst, target, is_self):
        @pl.loop(0, n)
        def _(i):
            p = order(i)
            mine = is_self(p)

            @pl.when(mine)
            def _():
                pltpu.make_async_copy(src(p), dst, recv_sem.at[k]).start()

            @pl.when(jnp.logical_not(mine))
            def _():
                copy_out(k, src(p), dst, target(p)).start()

    def finish(k, ref):
        pltpu.make_async_copy(ref, ref, recv_sem.at[k]).wait()

    def rows_of(ref, count):
        return lambda p: ref.at[pl.ds(count * p, count)]

    loads[0].wait()
    high, low = split(f_v[...])
    zero = jnp.zeros_like(high)

    def apart(x):
        return jnp.concatenate(
            [jnp.concatenate([x, zero], 1), jnp.concatenate([zero, x], 1)], 0
        )

    rhs_high = apart(high)
    table_loads[0].wait()
    table_loads[1].wait()
    out = dot(tables[0][...], jnp.concatenate([rhs_high, apart(low)], 0), NT)
    send1[...] = out[:, :128] + out[:, 128:] + dot(tables[1][...], rhs_high, NT)

    pl.semaphore_wait(barrier, greeted)
    scatter(
        0, GS, lambda i: space_peer(vs, i), rows_of(send1, W), recv1.at[pl.ds(W * s, W)],
        lambda p: swap(m, p), lambda p: jnp.logical_and(vm == m, p == vs),
    )

    for copy in loads[1:]:
        copy.wait()

    @pl.when(jnp.logical_and(vm == m, vs == s))
    def _():
        pltpu.make_async_copy(drive_in, drive, recv_sem.at[10]).start()

    @pl.when(jnp.logical_or(vm != m, vs != s))
    def _():
        copy_out(10, drive_in, drive, (vm, vs)).start()

    tail = pl.ds(KEEP, 8)
    recv1[tail, :] = jnp.zeros((8, 128), F32)
    recv3[tail, :] = jnp.zeros((8, 128), F32)
    columns = lax.broadcasted_iota(jnp.int32, (N, 128), 0) + m * N

    def tally(i, total):
        cell = probes_v[pl.ds(i, 1), :]
        obs = obs_v[pl.ds(i, 1), :]
        a, rest_ = split(obs)
        left = obs - a.astype(F32)
        b = left.astype(BF16)
        c = (left - b.astype(F32)).astype(BF16)
        ones = jnp.ones((1, 128), BF16)
        lhs = jnp.concatenate([ones, a, b, c], 0)
        hit = jnp.where(columns == cell, 1.0, 0.0).astype(BF16)
        return total + dot(lhs, hit, NT)

    total = lax.fori_loop(0, 16, tally, jnp.zeros((4, N), F32))
    sums = total[1:2] + total[2:3] + total[3:4]
    for i in range(4):
        hist_s[i : i + 1, :] = total[0:1, 128 * i : 128 * i + 128]
        hist_s[4 + i : 5 + i, :] = sums[:, 128 * i : 128 * i + 128]

    @pl.when(jnp.logical_and(vm == m, vs == s))
    def _():
        pltpu.make_async_copy(hist_s, hist_r, recv_sem.at[11]).start()

    @pl.when(jnp.logical_or(vm != m, vs != s))
    def _():
        copy_out(11, hist_s, hist_r, (vm, vs)).start()

    weights = mix_v[...]
    weights = weights + (1.0 - jnp.sum(weights, 0, keepdims=True)) * (1.0 / MEMBERS)
    weights = weights.T
    w_high, w_rest = split(weights)
    w_left = weights - w_high.astype(F32)
    w_mid = w_left.astype(BF16)
    w_low = (w_left - w_mid.astype(F32)).astype(BF16)
    w_parts = jnp.concatenate([w_high, w_mid, w_low], 0)
    for copy in table_loads[2:]:
        copy.wait()

    scale = 2.0 * math.pi / N
    slot = lax.broadcasted_iota(jnp.int32, (16, QP), 1)
    slot = jnp.where(slot < KEEP, slot, jnp.where(slot < 2 * KEEP, slot - 2 * KEEP, 0))
    wave_x = slot.astype(F32) * scale
    wave_y = (lax.broadcasted_iota(jnp.int32, (16, QP), 0) + vs * W).astype(F32) * scale
    squared = wave_x * wave_x + wave_y * wave_y
    inverse = jnp.where(squared > 0, 1.0 / jnp.where(squared > 0, squared, 1.0), 0.0)

    def for_all(x):
        return jnp.concatenate([x] * 4, 0)

    finish(0, recv1.at[pl.ds(0, KEEP)])
    w = to_slots(gather_columns(recv1), tables[2][...], tables[3][...])
    spectrum[...] = w
    iw = times_i(w)
    pairs = [(wave_y * inverse, -wave_x * inverse), (wave_x, wave_y)]
    for h, pair in enumerate(pairs):
        lhs = jnp.concatenate(
            [jnp.concatenate([for_all(u) * iw, for_all(u) * -w], 1) for u in pair], 0
        )
        e = to_cells(lhs, tables[4][...], tables[5][...])
        parts = [stack_lanes(e[32 * g : 32 * g + 32]) for g in range(4)]
        for slot_ in range(4):
            got = pick_groups([turn(parts[g], g - slot_) for g in range(4)])
            for hi in range(4):
                for c in range(2):
                    send2[h, pl.ds(2 * W * (4 * hi + slot_) + W * c, W), :] = got[
                        32 * hi + 16 * c : 32 * hi + 16 * c + W
                    ]
        exchange(1 + h, rows_of(send2.at[h], 2 * W), rows_of(recv2.at[h], 2 * W), "space")

    def to_rows(h):
        high, low = split(recv2[h])
        out = dot(tables[6][...], jnp.concatenate([high, low], 1))
        return out[:, :128] + out[:, 128:] + dot(tables[7][...], high)

    finish(1, recv2.at[0])
    velocity = to_rows(0)
    finish(2, recv2.at[1])
    product = velocity * to_rows(1)
    product = product + pltpu.roll(product, 64, 1)
    first = lax.broadcasted_iota(jnp.int32, product.shape, 1) < 64
    rhs = jnp.concatenate([jnp.where(first, product, 0.0), jnp.where(first, 0.0, product)], 0)
    high, low = split(rhs)
    out = dot(tables[0][...], jnp.concatenate([high, low], 1))
    send3[...] = out[:, :128] + out[:, 128:] + dot(tables[1][...], high)
    exchange(3, rows_of(send3, W), rows_of(recv3, W), "space")

    finish(3, recv3.at[pl.ds(0, KEEP)])
    adv = to_slots(gather_columns(recv3), tables[2][...], tables[3][...])
    w = spectrum[...]
    new = w + DT_STEP * (-adv - VISCOSITY * for_all(squared) * w)
    e = to_cells(jnp.concatenate([new, times_i(new)], 1), tables[4][...], tables[5][...])
    parts = {
        c * 2 + k: stack_lanes(e[32 * k + 16 * c : 32 * k + 16 * c + 16])
        for k in range(2) for c in range(2)
    }
    for slot_ in range(4):
        got = pick_groups([turn(parts[g], g - slot_) for g in range(4)])
        for hi in range(4):
            send4[pl.ds(W * (4 * hi + slot_), W), :] = got[16 * hi : 16 * hi + W]
    exchange(4, rows_of(send4, W), rows_of(recv4, W), "space")

    finish(10, drive)
    finish(11, hist_r)
    forcing = DT_STEP * drive[...]
    counts = jnp.concatenate([hist_r[i : i + 1, :] for i in range(4)], 1)
    obs_sums = jnp.concatenate([hist_r[4 + i : 5 + i, :] for i in range(4)], 1)

    finish(4, recv4)
    modes = recv4[...].T
    high, low = split(modes)
    out = dot(jnp.concatenate([high[:64], low[:64]], 0), tables[8][...])
    out = out + dot(jnp.concatenate([high[64:], low[64:]], 0), tables[10][...])
    fresh = out[:64] + out[64:] + dot(high[:64], tables[9][...]) + dot(high[64:], tables[11][...])
    fresh = fresh + jnp.concatenate([forcing, forcing], 0)
    for k in range(2):
        for i in range(4):
            by_row[:, 4 * k + i, :] = fresh[32 * k : 32 * k + 32, 128 * i : 128 * i + 128]
    send5[...] = by_row[...].astype(BF16)
    exchange(5, lambda p: send5.at[p], lambda p: recv5.at[p], "member")

    finish(5, recv5)
    by_member[...] = recv5[...].astype(F32)
    for k in range(2):
        for i in range(4):
            members_v[i, pl.ds(k, 32, stride=2), :] = by_member[:, 4 * k + i, :]
    values = jnp.concatenate([members_v[i] for i in range(4)], 1)

    centre = jnp.sum(values, 0, keepdims=True) * (1.0 / MEMBERS)
    anomaly = values - centre
    innovation = obs_sums - counts * centre
    other = jnp.concatenate(
        [anomaly * counts, innovation, jnp.zeros((63, N), F32)], 0
    )
    a_high, a_low = split(anomaly)
    b_high, b_low = split(other)
    send_a[...] = dot(a_high, b_high, NT) + dot(a_high, b_low, NT) + dot(a_low, b_high, NT)
    exchange(7, rows_of(send_a, 4), rows_of(recv_a, 4), "space")

    mixed = dot(w_parts, values.astype(BF16))
    mixed = mixed[:64] + mixed[64:128] + mixed[128:]
    for i in range(4):
        mixed_v[i] = mixed[:, 128 * i : 128 * i + 128]
    for k in range(2):
        for i in range(4):
            send6[:, 4 * k + i, :] = mixed_v[i, pl.ds(k, 32, stride=2), :]
    finish(7, recv_a)
    chunk = recv_a[pl.ds(0, 4), :]
    for p in range(1, GS):
        chunk = chunk + recv_a[pl.ds(4 * p, 4), :]
    send_b[...] = chunk
    exchange(8, lambda p: send_b, rows_of(recv_b, 4), "member")

    scatter(
        6, GM, lambda i: member_peer(vm, i), lambda p: send6.at[p], recv6.at[vm],
        lambda p: (p, vs), lambda p: jnp.logical_and(vs == s, p == m),
    )

    finish(8, recv_b)
    chunk = recv_b[pl.ds(0, 4), :]
    for p in range(1, GM):
        chunk = chunk + recv_b[pl.ds(4 * p, 4), :]
    send_c[...] = chunk
    exchange(9, lambda p: send_c, rows_of(recv_c, 4), "space")
    finish(6, recv6)
    rows_out[...] = recv6[...]

    finish(9, recv_c)
    sums_out[...] = recv_c[...]

    others = {
        0: send1.at[pl.ds(0, W * (GS - 1))],
        1: send2.at[0, pl.ds(0, 2 * W * (GS - 1))],
        2: send2.at[1, pl.ds(0, 2 * W * (GS - 1))],
        3: send3.at[pl.ds(0, W * (GS - 1))],
        4: send4.at[pl.ds(0, W * (GS - 1))],
        5: send5.at[pl.ds(0, GM - 1)],
        6: send6.at[pl.ds(0, GM - 1)],
        7: send_a.at[pl.ds(0, 4 * (GS - 1))],
        8: recv_b.at[pl.ds(0, 4 * (GM - 1))],
        9: recv_c.at[pl.ds(0, 4 * (GS - 1))],
    }

    def sent(k, ref):
        pltpu.make_async_copy(ref, ref, send_sem.at[k]).wait()

    for k, ref in others.items():
        sent(k, ref)

    @pl.when(vm != m)
    def _():
        sent(0, send1.at[pl.ds(0, W)])

    @pl.when(vs != s)
    def _():
        sent(6, send6.at[0])

    @pl.when(jnp.logical_or(vm != m, vs != s))
    def _():
        sent(10, drive_in)
        sent(11, hist_s)


def finish_kernel(rows, sums, analysis, spread, projection):
    for k in range(2):
        for i in range(4):
            analysis[k, :, pl.ds(128 * i, 128)] = rows[:, 4 * k + i, :]
    full = sums[...]
    spread[...] = full[:, :64] * (1.0 / PROBES)
    shape = (64, 64)
    diagonal = lax.broadcasted_iota(jnp.int32, shape, 0) == lax.broadcasted_iota(jnp.int32, shape, 1)
    column = jnp.where(diagonal, full[:, 64:65], 0.0)
    projection[...] = jnp.sum(column, 0, keepdims=True) * (1.0 / math.sqrt(PROBES))


def on_device(swirls, driving, mixing, probes, observed):
    tables = [jnp.asarray(t) for t in make_tables()]
    vmem = pltpu.VMEM
    lanes = 128
    buffers = [
        (64, N), (ROWS, N), (ROWS, N), (64, 64),
    ]
    scratch = [vmem(shape, F32) for shape in buffers]
    scratch += [vmem((16, 128), jnp.int32), vmem((16, 128), F32)]
    for shape in TABLE_SHAPES:
        scratch += [vmem(shape, BF16)] * 2
    for shape in [
        (KEEP, lanes), (KEEP + 8, lanes),
        (2, 2 * KEEP, lanes), (2, 2 * KEEP, lanes),
        (KEEP, lanes), (KEEP + 8, lanes),
        (KEEP, lanes), (KEEP, lanes),
        (GM, 8, lanes, BF16), (GM, 8, lanes, BF16), (GM, 8, lanes), (GM, 8, lanes),
        (8, lanes), (8, lanes),
        (64, lanes), (64, lanes), (4, lanes), (4 * GM, lanes), (4, lanes), (64, lanes),
        (64, QP), (4, 64, lanes), (4, 64, lanes), (GM, 8, lanes), (GM, 8, lanes),
    ]:
        narrow = shape[-1] is BF16
        scratch.append(vmem(shape[:-1], BF16) if narrow else vmem(shape, F32))
    dma = pltpu.SemaphoreType.DMA
    scratch += [dma((5,)), dma((12,)), dma((12,)), dma((12,))]
    anywhere = pl.BlockSpec(memory_space=pl.ANY)
    rows, sums = pl.pallas_call(
        kernel,
        out_shape=[
            jax.ShapeDtypeStruct((GM, 8, lanes), F32),
            jax.ShapeDtypeStruct((64, lanes), F32),
        ],
        in_specs=[anywhere] * (5 + len(tables)),
        out_specs=[pl.BlockSpec(memory_space=pltpu.VMEM)] * 2,
        scratch_shapes=scratch,
        compiler_params=pltpu.CompilerParams(
            collective_id=0, has_side_effects=True, vmem_limit_bytes=60 * 2**20
        ),
    )(
        swirls.reshape(64, N), driving, mixing, probes.reshape(16, 128), observed.reshape(16, 128),
        *tables,
    )
    analysis, spread, projection = pl.pallas_call(
        finish_kernel,
        out_shape=[
            jax.ShapeDtypeStruct((2, ROWS, N), F32),
            jax.ShapeDtypeStruct((64, 64), F32),
            jax.ShapeDtypeStruct((1, 64), F32),
        ],
        in_specs=[pl.BlockSpec(memory_space=pltpu.VMEM)] * 2,
        out_specs=[pl.BlockSpec(memory_space=pltpu.VMEM)] * 3,
    )(rows, sums)
    return analysis, spread, projection.reshape(64)


def solution(mesh):
    return jax.shard_map(
        on_device,
        mesh=mesh,
        in_specs=(P("member", "space", None), P("space", None), P(), P("space"), P("space")),
        out_specs=(P("member", "space", None), P(), P()),
        check_vma=False,
    )
```

```python
import math

import jax
import jax.numpy as jnp
import ml_dtypes
import numpy as np
from jax import lax
from jax.experimental import pallas as pl
from jax.experimental.pallas import tpu as pltpu
from jax.sharding import PartitionSpec as P

N = 512
KEEP = 160
DT_STEP = 0.1
VISCOSITY = 0.05
MEMBERS = 64
ROWS = 32
PROBES = 32768
GM = 32
GS = 16
W = KEEP // GS
QP = 384

F32 = jnp.float32
BF16 = jnp.bfloat16
MESH = pl.DeviceIdType.MESH
NN = (((1,), (0,)), ((), ()))
NT = (((1,), (1,)), ((), ()))


def halves(table):
    high = table.astype(np.float32).astype(ml_dtypes.bfloat16)
    low = (table - high.astype(np.float64)).astype(np.float32).astype(ml_dtypes.bfloat16)
    return [high, low]


def make_tables():
    cells = np.arange(N)
    slots = np.arange(2 * KEEP)
    kx = np.where(slots < KEEP, slots, slots - 2 * KEEP)
    ky = np.arange(KEEP)

    def trig(a, b):
        angle = (a[:, None] * b[None, :] % N) * (2.0 * np.pi / N)
        return np.cos(angle), np.sin(angle)

    cos_y, sin_y = trig(ky, cells)
    rows_f = np.concatenate([cos_y, -sin_y], 1)
    cos_x, sin_x = trig(cells, kx)
    cols_f = np.zeros((2 * N, QP))
    cols_f[:N, : 2 * KEEP] = cos_x / (N * N)
    cols_f[N:, : 2 * KEEP] = sin_x / (N * N)
    cols_g = np.zeros((2 * QP, N))
    cols_g[: 2 * KEEP] = cos_x.T
    cols_g[QP : QP + 2 * KEEP] = sin_x.T
    count = np.where(ky == 0, 1.0, 2.0)[:, None]
    rows_g4 = np.stack([cos_y * count, -sin_y * count], 0)
    rows_g4 = rows_g4.reshape(2, GS, W, N).transpose(1, 0, 2, 3).reshape(2 * KEEP, N).T
    out = []
    for t in (rows_f, cols_f, cols_g, rows_g4, cos_y * count, -sin_y * count):
        out += halves(np.ascontiguousarray(t))
    return out


TABLE_SHAPES = [(KEEP, 2 * N), (2 * N, QP), (2 * QP, N), (N, 2 * KEEP), (KEEP, N), (KEEP, N)]


def dot(a, b, dims=NN):
    return lax.dot_general(a, b, dims, preferred_element_type=F32)


def split(x):
    high = x.astype(BF16)
    return high, (x - high.astype(F32)).astype(BF16)


def hops(step, ring):
    return min(step, ring - step)


NEAR = sorted(
    ((dx, a, b) for dx in range(4) for a in range(2) for b in range(2)),
    key=lambda d: (-hops(d[0], 4) - d[1], -d[2]),
)
FAR = sorted(
    ((dy, dz) for dy in range(8) for dz in range(4)),
    key=lambda d: (-hops(d[0], 8) - 2 * hops(d[1], 4), -d[0]),
)
BACK = sorted(
    ((dy, a, b) for dy in range(8) for a in range(2) for b in range(2)),
    key=lambda d: (-hops(d[0], 8), -d[1], -d[2]),
)


def lane_group(shape):
    return lax.div(lax.broadcasted_iota(jnp.int32, shape, len(shape) - 1), 32)


def pick_groups(pieces):
    group = lane_group(pieces[0].shape)
    low = jnp.where(group == 0, pieces[0], pieces[1])
    high = jnp.where(group == 2, pieces[2], pieces[3])
    return jnp.where(group < 2, low, high)


def turn(x, groups):
    groups %= 4
    return x if groups == 0 else pltpu.roll(x, 32 * groups, 1)


def gather_columns(recv):
    by_slot = [
        jnp.concatenate([recv[pl.ds(W * (4 * hi + slot), 16), :] for hi in range(4)], 0)
        for slot in range(4)
    ]
    rows = []
    for m in range(2):
        for c in range(2):
            t = c * 2 + m
            got = pick_groups([turn(by_slot[slot], slot - t) for slot in range(4)])
            rows.append(jnp.concatenate([got[16 * hi : 16 * hi + 16] for hi in range(4)], 1))
    return jnp.concatenate(rows, 0)


def times_i(w):
    return jnp.concatenate([-w[16:32], w[0:16], -w[48:64], w[32:48]], 0)


def to_slots(d, t_high, t_low):
    both = jnp.concatenate([d, -times_i(d)], 1)
    high, low = split(both)
    out = dot(jnp.concatenate([high, low], 0), t_high)
    return out[:64] + out[64:] + dot(high, t_low)


def to_cells(lhs, t_high, t_low):
    rows = lhs.shape[0]
    high, low = split(lhs)
    out = dot(jnp.concatenate([high, low], 0), t_high)
    return out[:rows] + out[rows:] + dot(high, t_low)


def stack_lanes(x):
    return jnp.concatenate([x[:, 128 * i : 128 * i + 128] for i in range(4)], 0)


def kernel(
    swirls, driving, mixing, probes, observed, *rest
):
    tables_hbm = rest[:12]
    rows_out, sums_out = rest[12:14]
    (
        f_v, drive_in, drive, mix_v, probes_v, obs_v,
        *more
    ) = rest[14:]
    tables = more[:12]
    (
        send1, recv1, send2, recv2, send3, recv3, send4, recv4, send5, recv5, send6, recv6,
        hist_s, hist_r, send_a, recv_a, send_b, recv_b, send_c, recv_c,
        spectrum, members_v, mixed_v, by_row, by_member,
        load_sem, table_sem, send_sem, recv_sem,
    ) = more[12:]
    m, s = lax.axis_index("member"), lax.axis_index("space")
    x, z_hi = lax.div(s, 4), lax.rem(s, 4)
    z_lo, y, core = lax.div(m, 16), lax.rem(lax.div(m, 2), 8), lax.rem(m, 2)
    hi_hi, hi_lo = lax.div(z_hi, 2), lax.rem(z_hi, 2)
    pair = z_lo * 2 + core
    vm, vs = hi_hi * 16 + y * 2 + hi_lo, x * 4 + pair
    fixed = z_hi == pair
    moved = z_hi != pair
    xs = [x] + [lax.rem(x + d, 4) for d in range(1, 4)]
    ys = [y] + [lax.rem(y + d, 8) for d in range(1, 8)]
    zs = [z_hi] + [lax.rem(z_hi + d, 4) for d in range(1, 4)]
    lows, cores = [z_lo, 1 - z_lo], [core, 1 - core]
    near_m = {(a, b): lows[a] * 16 + y * 2 + cores[b] for a in range(2) for b in range(2)}
    back_m = [lows[0] * 16, lows[1] * 16]
    z_m = [lax.div(z, 2) * 16 + lax.rem(z, 2) for z in zs]

    def near_peer(d):
        return xs[d[0]] * 4 + lows[d[1]] * 2 + cores[d[2]]

    def near_device(d, z):
        return near_m[d[1], d[2]], xs[d[0]] * 4 + z

    def far_peer(d):
        return z_m[d[1]] + ys[d[0]] * 2

    def far_device(d, low, core_):
        return low * 16 + ys[d[0]] * 2 + core_, x * 4 + zs[d[1]]

    def back_peer(d):
        return back_m[d[1]] + ys[d[0]] * 2 + cores[d[2]]

    def there(target):
        return dict(device_id={"member": target[0], "space": target[1]}, device_id_type=MESH)

    barrier = pltpu.get_barrier_semaphore()

    def hello(target):
        pl.semaphore_signal(barrier, inc=1, **there(target))

    for d in FAR[:-1]:
        hello(far_device(d, z_lo, core))
        hello(far_device(d, hi_hi, hi_lo))
    for dx, dz in [(2, 2), (2, 1), (2, 3), (1, 2), (3, 2), (2, 0), (0, 2), (1, 1), (1, 3), (3, 1), (3, 3), (1, 0), (3, 0), (0, 1), (0, 3)]:
        hello((vm, xs[dx] * 4 + zs[dz]))
    for d in NEAR[:-1]:
        hello(near_device(d, z_hi))

    @pl.when(moved)
    def _():
        hello(far_device(FAR[-1], hi_hi, hi_lo))
        hello((vm, s))

    greeted = 2 * (GS + GM - 2) + 2 * moved.astype(jnp.int32)

    loads = [
        pltpu.make_async_copy(src, dst, load_sem.at[i])
        for i, (src, dst) in enumerate(
            [(swirls, f_v), (driving, drive_in), (mixing, mix_v), (probes, probes_v), (observed, obs_v)]
        )
    ]
    table_loads = [
        pltpu.make_async_copy(src, dst, table_sem.at[i])
        for i, (src, dst) in enumerate(zip(tables_hbm, tables))
    ]
    loads[0].start()
    for copy in table_loads[:2]:
        copy.start()
    for copy in loads[1:]:
        copy.start()
    for copy in table_loads[2:]:
        copy.start()

    def copy_out(k, src, dst, target):
        return pltpu.make_async_remote_copy(
            src_ref=src, dst_ref=dst, send_sem=send_sem.at[k], recv_sem=recv_sem.at[k], **there(target)
        )

    def exchange(k, src, dst, axis):
        me = vs if axis == "space" else vm
        for d in NEAR[:-1] if axis == "space" else FAR[:-1]:
            if axis == "space":
                p, target = near_peer(d), near_device(d, z_hi)
            else:
                p, target = far_peer(d), far_device(d, z_lo, core)
            copy_out(k, src(p), dst(me), target).start()
        pltpu.make_async_copy(src(me), dst(me), recv_sem.at[k]).start()

    def scatter(k, steps, peer, device, src, dst):
        for d in steps[:-1]:
            copy_out(k, src(peer(d)), dst, device(d)).start()
        p = peer(steps[-1])

        @pl.when(fixed)
        def _():
            pltpu.make_async_copy(src(p), dst, recv_sem.at[k]).start()

        @pl.when(moved)
        def _():
            copy_out(k, src(p), dst, device(steps[-1])).start()

    def finish(k, ref):
        pltpu.make_async_copy(ref, ref, recv_sem.at[k]).wait()

    def rows_of(ref, count):
        return lambda p: ref.at[pl.ds(count * p, count)]

    loads[0].wait()
    high, low = split(f_v[...])
    zero = jnp.zeros_like(high)

    def apart(x):
        return jnp.concatenate(
            [jnp.concatenate([x, zero], 1), jnp.concatenate([zero, x], 1)], 0
        )

    rhs_high = apart(high)
    table_loads[0].wait()
    table_loads[1].wait()
    out = dot(tables[0][...], jnp.concatenate([rhs_high, apart(low)], 0), NT)
    send1[...] = out[:, :128] + out[:, 128:] + dot(tables[1][...], rhs_high, NT)

    pl.semaphore_wait(barrier, greeted)
    scatter(
        0, NEAR, near_peer, lambda d: near_device(d, pair), rows_of(send1, W), recv1.at[pl.ds(W * s, W)]
    )

    for copy in loads[1:]:
        copy.wait()

    @pl.when(fixed)
    def _():
        pltpu.make_async_copy(drive_in, drive, recv_sem.at[10]).start()

    @pl.when(moved)
    def _():
        copy_out(10, drive_in, drive, (vm, vs)).start()

    tail = pl.ds(KEEP, 8)
    recv1[tail, :] = jnp.zeros((8, 128), F32)
    recv3[tail, :] = jnp.zeros((8, 128), F32)
    columns = lax.broadcasted_iota(jnp.int32, (N, 128), 0) + m * N

    def tally(i, total):
        cell = probes_v[pl.ds(i, 1), :]
        obs = obs_v[pl.ds(i, 1), :]
        a, rest_ = split(obs)
        left = obs - a.astype(F32)
        b = left.astype(BF16)
        c = (left - b.astype(F32)).astype(BF16)
        ones = jnp.ones((1, 128), BF16)
        lhs = jnp.concatenate([ones, a, b, c], 0)
        hit = jnp.where(columns == cell, 1.0, 0.0).astype(BF16)
        return total + dot(lhs, hit, NT)

    total = lax.fori_loop(0, 16, tally, jnp.zeros((4, N), F32))
    sums = total[1:2] + total[2:3] + total[3:4]
    for i in range(4):
        hist_s[i : i + 1, :] = total[0:1, 128 * i : 128 * i + 128]
        hist_s[4 + i : 5 + i, :] = sums[:, 128 * i : 128 * i + 128]

    @pl.when(fixed)
    def _():
        pltpu.make_async_copy(hist_s, hist_r, recv_sem.at[11]).start()

    @pl.when(moved)
    def _():
        copy_out(11, hist_s, hist_r, (vm, vs)).start()

    weights = mix_v[...]
    weights = weights + (1.0 - jnp.sum(weights, 0, keepdims=True)) * (1.0 / MEMBERS)
    weights = weights.T
    w_high, w_rest = split(weights)
    w_left = weights - w_high.astype(F32)
    w_mid = w_left.astype(BF16)
    w_low = (w_left - w_mid.astype(F32)).astype(BF16)
    w_parts = jnp.concatenate([w_high, w_mid, w_low], 0)
    for copy in table_loads[2:]:
        copy.wait()

    scale = 2.0 * math.pi / N
    slot = lax.broadcasted_iota(jnp.int32, (16, QP), 1)
    slot = jnp.where(slot < KEEP, slot, jnp.where(slot < 2 * KEEP, slot - 2 * KEEP, 0))
    wave_x = slot.astype(F32) * scale
    wave_y = (lax.broadcasted_iota(jnp.int32, (16, QP), 0) + vs * W).astype(F32) * scale
    squared = wave_x * wave_x + wave_y * wave_y
    inverse = jnp.where(squared > 0, 1.0 / jnp.where(squared > 0, squared, 1.0), 0.0)

    def for_all(x):
        return jnp.concatenate([x] * 4, 0)

    finish(0, recv1.at[pl.ds(0, KEEP)])
    w = to_slots(gather_columns(recv1), tables[2][...], tables[3][...])
    spectrum[...] = w
    iw = times_i(w)
    pairs = [(wave_y * inverse, -wave_x * inverse), (wave_x, wave_y)]
    for h, pair in enumerate(pairs):
        lhs = jnp.concatenate(
            [jnp.concatenate([for_all(u) * iw, for_all(u) * -w], 1) for u in pair], 0
        )
        e = to_cells(lhs, tables[4][...], tables[5][...])
        parts = [stack_lanes(e[32 * g : 32 * g + 32]) for g in range(4)]
        for slot_ in range(4):
            got = pick_groups([turn(parts[g], g - slot_) for g in range(4)])
            for hi in range(4):
                for c in range(2):
                    send2[h, pl.ds(2 * W * (4 * hi + slot_) + W * c, W), :] = got[
                        32 * hi + 16 * c : 32 * hi + 16 * c + W
                    ]
        exchange(1 + h, rows_of(send2.at[h], 2 * W), rows_of(recv2.at[h], 2 * W), "space")

    def to_rows(h):
        high, low = split(recv2[h])
        out = dot(tables[6][...], jnp.concatenate([high, low], 1))
        return out[:, :128] + out[:, 128:] + dot(tables[7][...], high)

    finish(1, recv2.at[0])
    velocity = to_rows(0)
    finish(2, recv2.at[1])
    product = velocity * to_rows(1)
    product = product + pltpu.roll(product, 64, 1)
    first = lax.broadcasted_iota(jnp.int32, product.shape, 1) < 64
    rhs = jnp.concatenate([jnp.where(first, product, 0.0), jnp.where(first, 0.0, product)], 0)
    high, low = split(rhs)
    out = dot(tables[0][...], jnp.concatenate([high, low], 1))
    send3[...] = out[:, :128] + out[:, 128:] + dot(tables[1][...], high)
    exchange(3, rows_of(send3, W), rows_of(recv3, W), "space")

    finish(3, recv3.at[pl.ds(0, KEEP)])
    adv = to_slots(gather_columns(recv3), tables[2][...], tables[3][...])
    w = spectrum[...]
    new = w + DT_STEP * (-adv - VISCOSITY * for_all(squared) * w)
    e = to_cells(jnp.concatenate([new, times_i(new)], 1), tables[4][...], tables[5][...])
    parts = {
        c * 2 + k: stack_lanes(e[32 * k + 16 * c : 32 * k + 16 * c + 16])
        for k in range(2) for c in range(2)
    }
    for slot_ in range(4):
        got = pick_groups([turn(parts[g], g - slot_) for g in range(4)])
        for hi in range(4):
            send4[pl.ds(W * (4 * hi + slot_), W), :] = got[16 * hi : 16 * hi + W]
    exchange(4, rows_of(send4, W), rows_of(recv4, W), "space")

    finish(10, drive)
    finish(11, hist_r)
    forcing = DT_STEP * drive[...]
    counts = jnp.concatenate([hist_r[i : i + 1, :] for i in range(4)], 1)
    obs_sums = jnp.concatenate([hist_r[4 + i : 5 + i, :] for i in range(4)], 1)

    finish(4, recv4)
    modes = recv4[...].T
    high, low = split(modes)
    out = dot(jnp.concatenate([high[:64], low[:64]], 0), tables[8][...])
    out = out + dot(jnp.concatenate([high[64:], low[64:]], 0), tables[10][...])
    fresh = out[:64] + out[64:] + dot(high[:64], tables[9][...]) + dot(high[64:], tables[11][...])
    fresh = fresh + jnp.concatenate([forcing, forcing], 0)
    for k in range(2):
        for i in range(4):
            by_row[:, 4 * k + i, :] = fresh[32 * k : 32 * k + 32, 128 * i : 128 * i + 128]
    send5[...] = by_row[...].astype(BF16)
    exchange(5, lambda p: send5.at[p], lambda p: recv5.at[p], "member")

    finish(5, recv5)
    by_member[...] = recv5[...].astype(F32)
    for k in range(2):
        for i in range(4):
            members_v[i, pl.ds(k, 32, stride=2), :] = by_member[:, 4 * k + i, :]
    values = jnp.concatenate([members_v[i] for i in range(4)], 1)

    centre = jnp.sum(values, 0, keepdims=True) * (1.0 / MEMBERS)
    anomaly = values - centre
    innovation = obs_sums - counts * centre
    other = jnp.concatenate(
        [anomaly * counts, innovation, jnp.zeros((63, N), F32)], 0
    )
    a_high, a_low = split(anomaly)
    b_high, b_low = split(other)
    send_a[...] = dot(a_high, b_high, NT) + dot(a_high, b_low, NT) + dot(a_low, b_high, NT)
    exchange(7, rows_of(send_a, 4), rows_of(recv_a, 4), "space")

    mixed = dot(w_parts, values.astype(BF16))
    mixed = mixed[:64] + mixed[64:128] + mixed[128:]
    for i in range(4):
        mixed_v[i] = mixed[:, 128 * i : 128 * i + 128]
    for k in range(2):
        for i in range(4):
            send6[:, 4 * k + i, :] = mixed_v[i, pl.ds(k, 32, stride=2), :]
    finish(7, recv_a)
    chunk = recv_a[pl.ds(0, 4), :]
    for p in range(1, GS):
        chunk = chunk + recv_a[pl.ds(4 * p, 4), :]
    send_b[...] = chunk
    exchange(8, lambda p: send_b, rows_of(recv_b, 4), "member")

    scatter(
        6, BACK, back_peer, lambda d: (back_peer(d), vs), lambda p: send6.at[p], recv6.at[vm]
    )

    finish(8, recv_b)
    chunk = recv_b[pl.ds(0, 4), :]
    for p in range(1, GM):
        chunk = chunk + recv_b[pl.ds(4 * p, 4), :]
    send_c[...] = chunk
    exchange(9, lambda p: send_c, rows_of(recv_c, 4), "space")
    finish(6, recv6)
    rows_out[...] = recv6[...]

    finish(9, recv_c)
    sums_out[...] = recv_c[...]

    others = {
        0: send1.at[pl.ds(0, W * (GS - 1))],
        1: send2.at[0, pl.ds(0, 2 * W * (GS - 1))],
        2: send2.at[1, pl.ds(0, 2 * W * (GS - 1))],
        3: send3.at[pl.ds(0, W * (GS - 1))],
        4: send4.at[pl.ds(0, W * (GS - 1))],
        5: send5.at[pl.ds(0, GM - 1)],
        6: send6.at[pl.ds(0, GM - 1)],
        7: send_a.at[pl.ds(0, 4 * (GS - 1))],
        8: recv_b.at[pl.ds(0, 4 * (GM - 1))],
        9: recv_c.at[pl.ds(0, 4 * (GS - 1))],
    }

    def sent(k, ref):
        pltpu.make_async_copy(ref, ref, send_sem.at[k]).wait()

    for k, ref in others.items():
        sent(k, ref)

    @pl.when(moved)
    def _():
        sent(0, send1.at[pl.ds(0, W)])

    @pl.when(moved)
    def _():
        sent(6, send6.at[0])

    @pl.when(moved)
    def _():
        sent(10, drive_in)
        sent(11, hist_s)


def finish_kernel(rows, sums, analysis, spread, projection):
    for k in range(2):
        for i in range(4):
            analysis[k, :, pl.ds(128 * i, 128)] = rows[:, 4 * k + i, :]
    full = sums[...]
    spread[...] = full[:, :64] * (1.0 / PROBES)
    shape = (64, 64)
    diagonal = lax.broadcasted_iota(jnp.int32, shape, 0) == lax.broadcasted_iota(jnp.int32, shape, 1)
    column = jnp.where(diagonal, full[:, 64:65], 0.0)
    projection[...] = jnp.sum(column, 0, keepdims=True) * (1.0 / math.sqrt(PROBES))


def on_device(swirls, driving, mixing, probes, observed):
    tables = [jnp.asarray(t) for t in make_tables()]
    vmem = pltpu.VMEM
    lanes = 128
    buffers = [
        (64, N), (ROWS, N), (ROWS, N), (64, 64),
    ]
    scratch = [vmem(shape, F32) for shape in buffers]
    scratch += [vmem((16, 128), jnp.int32), vmem((16, 128), F32)]
    for shape in TABLE_SHAPES:
        scratch += [vmem(shape, BF16)] * 2
    for shape in [
        (KEEP, lanes), (KEEP + 8, lanes),
        (2, 2 * KEEP, lanes), (2, 2 * KEEP, lanes),
        (KEEP, lanes), (KEEP + 8, lanes),
        (KEEP, lanes), (KEEP, lanes),
        (GM, 8, lanes, BF16), (GM, 8, lanes, BF16), (GM, 8, lanes), (GM, 8, lanes),
        (8, lanes), (8, lanes),
        (64, lanes), (64, lanes), (4, lanes), (4 * GM, lanes), (4, lanes), (64, lanes),
        (64, QP), (4, 64, lanes), (4, 64, lanes), (GM, 8, lanes), (GM, 8, lanes),
    ]:
        narrow = shape[-1] is BF16
        scratch.append(vmem(shape[:-1], BF16) if narrow else vmem(shape, F32))
    dma = pltpu.SemaphoreType.DMA
    scratch += [dma((5,)), dma((12,)), dma((12,)), dma((12,))]
    anywhere = pl.BlockSpec(memory_space=pl.ANY)
    rows, sums = pl.pallas_call(
        kernel,
        out_shape=[
            jax.ShapeDtypeStruct((GM, 8, lanes), F32),
            jax.ShapeDtypeStruct((64, lanes), F32),
        ],
        in_specs=[anywhere] * (5 + len(tables)),
        out_specs=[pl.BlockSpec(memory_space=pltpu.VMEM)] * 2,
        scratch_shapes=scratch,
        compiler_params=pltpu.CompilerParams(
            collective_id=0, has_side_effects=True, vmem_limit_bytes=60 * 2**20
        ),
    )(
        swirls.reshape(64, N), driving, mixing, probes.reshape(16, 128), observed.reshape(16, 128),
        *tables,
    )
    analysis, spread, projection = pl.pallas_call(
        finish_kernel,
        out_shape=[
            jax.ShapeDtypeStruct((2, ROWS, N), F32),
            jax.ShapeDtypeStruct((64, 64), F32),
            jax.ShapeDtypeStruct((1, 64), F32),
        ],
        in_specs=[pl.BlockSpec(memory_space=pltpu.VMEM)] * 2,
        out_specs=[pl.BlockSpec(memory_space=pltpu.VMEM)] * 3,
    )(rows, sums)
    return analysis, spread, projection.reshape(64)


def solution(mesh):
    return jax.shard_map(
        on_device,
        mesh=mesh,
        in_specs=(P("member", "space", None), P("space", None), P(), P("space"), P("space")),
        out_specs=(P("member", "space", None), P(), P()),
        check_vma=False,
    )
```

```python
import math

import jax
import jax.numpy as jnp
import ml_dtypes
import numpy as np
from jax import lax
from jax.experimental import pallas as pl
from jax.experimental.pallas import tpu as pltpu
from jax.sharding import PartitionSpec as P

N = 512
KEEP = 160
DT_STEP = 0.1
VISCOSITY = 0.05
MEMBERS = 64
ROWS = 32
PROBES = 32768
GM = 32
GS = 16
W = KEEP // GS
QP = 384

F32 = jnp.float32
BF16 = jnp.bfloat16
MESH = pl.DeviceIdType.MESH
NN = (((1,), (0,)), ((), ()))
NT = (((1,), (1,)), ((), ()))


def halves(table):
    high = table.astype(np.float32).astype(ml_dtypes.bfloat16)
    low = (table - high.astype(np.float64)).astype(np.float32).astype(ml_dtypes.bfloat16)
    return [high, low]


def make_tables():
    cells = np.arange(N)
    slots = np.arange(2 * KEEP)
    kx = np.where(slots < KEEP, slots, slots - 2 * KEEP)
    ky = np.arange(KEEP)

    def trig(a, b):
        angle = (a[:, None] * b[None, :] % N) * (2.0 * np.pi / N)
        return np.cos(angle), np.sin(angle)

    cos_y, sin_y = trig(ky, cells)
    rows_f = np.concatenate([cos_y, -sin_y], 1)
    cos_x, sin_x = trig(cells, kx)
    cols_f = np.zeros((2 * N, QP))
    cols_f[:N, : 2 * KEEP] = cos_x / (N * N)
    cols_f[N:, : 2 * KEEP] = sin_x / (N * N)
    cols_g = np.zeros((2 * QP, N))
    cols_g[: 2 * KEEP] = cos_x.T
    cols_g[QP : QP + 2 * KEEP] = sin_x.T
    count = np.where(ky == 0, 1.0, 2.0)[:, None]
    rows_g4 = np.stack([cos_y * count, -sin_y * count], 0)
    rows_g4 = rows_g4.reshape(2, GS, W, N).transpose(1, 0, 2, 3).reshape(2 * KEEP, N).T
    out = []
    for t in (rows_f, cols_f, cols_g, rows_g4, cos_y * count, -sin_y * count):
        out += halves(np.ascontiguousarray(t))
    return out


TABLE_SHAPES = [(KEEP, 2 * N), (2 * N, QP), (2 * QP, N), (N, 2 * KEEP), (KEEP, N), (KEEP, N)]


def dot(a, b, dims=NN):
    return lax.dot_general(a, b, dims, preferred_element_type=F32)


def split(x):
    high = x.astype(BF16)
    return high, (x - high.astype(F32)).astype(BF16)


def hops(step, ring):
    return min(step, ring - step)


NEAR = sorted(
    ((dx, a, b) for dx in range(4) for a in range(2) for b in range(2)),
    key=lambda d: (-hops(d[0], 4) - d[1], -d[2]),
)
FAR = sorted(
    ((dy, dz) for dy in range(8) for dz in range(4)),
    key=lambda d: (-hops(d[0], 8) - 2 * hops(d[1], 4), -d[0]),
)
BACK = sorted(
    ((dy, a, b) for dy in range(8) for a in range(2) for b in range(2)),
    key=lambda d: (-hops(d[0], 8), -d[1], -d[2]),
)


def lane_group(shape):
    return lax.div(lax.broadcasted_iota(jnp.int32, shape, len(shape) - 1), 32)


def pick_groups(pieces):
    group = lane_group(pieces[0].shape)
    low = jnp.where(group == 0, pieces[0], pieces[1])
    high = jnp.where(group == 2, pieces[2], pieces[3])
    return jnp.where(group < 2, low, high)


def turn(x, groups):
    groups %= 4
    return x if groups == 0 else pltpu.roll(x, 32 * groups, 1)


def gather_columns(recv):
    by_slot = [
        jnp.concatenate([recv[pl.ds(W * (4 * hi + slot), 16), :] for hi in range(4)], 0)
        for slot in range(4)
    ]
    rows = []
    for m in range(2):
        for c in range(2):
            t = c * 2 + m
            got = pick_groups([turn(by_slot[slot], slot - t) for slot in range(4)])
            rows.append(jnp.concatenate([got[16 * hi : 16 * hi + 16] for hi in range(4)], 1))
    return jnp.concatenate(rows, 0)


def times_i(w):
    return jnp.concatenate([-w[16:32], w[0:16], -w[48:64], w[32:48]], 0)


def to_slots(d, t_high, t_low):
    both = jnp.concatenate([d, -times_i(d)], 1)
    high, low = split(both)
    out = dot(jnp.concatenate([high, low], 0), t_high)
    return out[:64] + out[64:] + dot(high, t_low)


def to_cells(lhs, t_high, t_low):
    rows = lhs.shape[0]
    high, low = split(lhs)
    out = dot(jnp.concatenate([high, low], 0), t_high)
    return out[:rows] + out[rows:] + dot(high, t_low)


def stack_lanes(x):
    return jnp.concatenate([x[:, 128 * i : 128 * i + 128] for i in range(4)], 0)


def kernel(
    swirls, driving, mixing, probes, observed, *rest
):
    tables_hbm = rest[:12]
    rows_out, sums_out = rest[12:14]
    (
        f_v, drive_in, drive, mix_v, probes_v, obs_v,
        *more
    ) = rest[14:]
    tables = more[:12]
    (
        send1, recv1, send2, recv2, send3, recv3, send4, recv4, send5, recv5, send6, recv6,
        hist_s, hist_r, send_a, recv_a, send_b, recv_b, send_c, recv_c,
        spectrum, members_v, mixed_v, by_row, by_member,
        load_sem, table_sem, send_sem, recv_sem, store_sem,
    ) = more[12:]
    m, s = lax.axis_index("member"), lax.axis_index("space")
    x, z_hi = lax.div(s, 4), lax.rem(s, 4)
    z_lo, y, core = lax.div(m, 16), lax.rem(lax.div(m, 2), 8), lax.rem(m, 2)
    hi_hi, hi_lo = lax.div(z_hi, 2), lax.rem(z_hi, 2)
    pair = z_lo * 2 + core
    vm, vs = hi_hi * 16 + y * 2 + hi_lo, x * 4 + pair
    fixed = z_hi == pair
    moved = z_hi != pair
    xs = [x] + [lax.rem(x + d, 4) for d in range(1, 4)]
    ys = [y] + [lax.rem(y + d, 8) for d in range(1, 8)]
    zs = [z_hi] + [lax.rem(z_hi + d, 4) for d in range(1, 4)]
    lows, cores = [z_lo, 1 - z_lo], [core, 1 - core]
    near_m = {(a, b): lows[a] * 16 + y * 2 + cores[b] for a in range(2) for b in range(2)}
    back_m = [lows[0] * 16, lows[1] * 16]
    z_m = [lax.div(z, 2) * 16 + lax.rem(z, 2) for z in zs]

    def near_peer(d):
        return xs[d[0]] * 4 + lows[d[1]] * 2 + cores[d[2]]

    def near_device(d, z):
        return near_m[d[1], d[2]], xs[d[0]] * 4 + z

    def far_peer(d):
        return z_m[d[1]] + ys[d[0]] * 2

    def far_device(d, low, core_):
        return low * 16 + ys[d[0]] * 2 + core_, x * 4 + zs[d[1]]

    def back_peer(d):
        return back_m[d[1]] + ys[d[0]] * 2 + cores[d[2]]

    def there(target):
        return dict(device_id={"member": target[0], "space": target[1]}, device_id_type=MESH)

    barrier = pltpu.get_barrier_semaphore()

    def hello(target):
        pl.semaphore_signal(barrier, inc=1, **there(target))

    for d in FAR[:-1]:
        hello(far_device(d, z_lo, core))
        hello(far_device(d, hi_hi, hi_lo))
    for dx, dz in [(2, 2), (2, 1), (2, 3), (1, 2), (3, 2), (2, 0), (0, 2), (1, 1), (1, 3), (3, 1), (3, 3), (1, 0), (3, 0), (0, 1), (0, 3)]:
        hello((vm, xs[dx] * 4 + zs[dz]))
    for d in NEAR[:-1]:
        hello(near_device(d, z_hi))

    @pl.when(moved)
    def _():
        hello(far_device(FAR[-1], hi_hi, hi_lo))
        hello((vm, s))

    greeted = 2 * (GS + GM - 2) + 2 * moved.astype(jnp.int32)

    loads = [
        pltpu.make_async_copy(src, dst, load_sem.at[i])
        for i, (src, dst) in enumerate(
            [(swirls, f_v), (driving, drive_in), (mixing, mix_v), (probes, probes_v), (observed, obs_v)]
        )
    ]
    table_loads = [
        pltpu.make_async_copy(src, dst, table_sem.at[i])
        for i, (src, dst) in enumerate(zip(tables_hbm, tables))
    ]
    loads[0].start()
    for copy in table_loads[:2]:
        copy.start()
    for copy in loads[1:]:
        copy.start()
    for copy in table_loads[2:]:
        copy.start()

    def copy_out(k, src, dst, target):
        return pltpu.make_async_remote_copy(
            src_ref=src, dst_ref=dst, send_sem=send_sem.at[k], recv_sem=recv_sem.at[k], **there(target)
        )

    def exchange(k, src, dst, axis):
        me = vs if axis == "space" else vm
        for d in NEAR[:-1] if axis == "space" else FAR[:-1]:
            if axis == "space":
                p, target = near_peer(d), near_device(d, z_hi)
            else:
                p, target = far_peer(d), far_device(d, z_lo, core)
            copy_out(k, src(p), dst(me), target).start()
        pltpu.make_async_copy(src(me), dst(me), recv_sem.at[k]).start()

    def scatter(k, steps, peer, device, src, dst):
        for d in steps[:-1]:
            copy_out(k, src(peer(d)), dst, device(d)).start()
        p = peer(steps[-1])

        @pl.when(fixed)
        def _():
            pltpu.make_async_copy(src(p), dst, recv_sem.at[k]).start()

        @pl.when(moved)
        def _():
            copy_out(k, src(p), dst, device(steps[-1])).start()

    def finish(k, ref):
        pltpu.make_async_copy(ref, ref, recv_sem.at[k]).wait()

    def rows_of(ref, count):
        return lambda p: ref.at[pl.ds(count * p, count)]

    loads[0].wait()
    high, low = split(f_v[...])
    zero = jnp.zeros_like(high)

    def apart(x):
        return jnp.concatenate(
            [jnp.concatenate([x, zero], 1), jnp.concatenate([zero, x], 1)], 0
        )

    rhs_high = apart(high)
    table_loads[0].wait()
    table_loads[1].wait()
    out = dot(tables[0][...], jnp.concatenate([rhs_high, apart(low)], 0), NT)
    send1[...] = out[:, :128] + out[:, 128:] + dot(tables[1][...], rhs_high, NT)

    pl.semaphore_wait(barrier, greeted)
    scatter(
        0, NEAR, near_peer, lambda d: near_device(d, pair), rows_of(send1, W), recv1.at[pl.ds(W * s, W)]
    )

    for copy in loads[1:]:
        copy.wait()
    tail = pl.ds(KEEP, 8)
    recv1[tail, :] = jnp.zeros((8, 128), F32)
    recv3[tail, :] = jnp.zeros((8, 128), F32)
    columns = lax.broadcasted_iota(jnp.int32, (N, 128), 0) + m * N

    def tally(i, total):
        cell = probes_v[pl.ds(i, 1), :]
        obs = obs_v[pl.ds(i, 1), :]
        a, rest_ = split(obs)
        left = obs - a.astype(F32)
        b = left.astype(BF16)
        c = (left - b.astype(F32)).astype(BF16)
        ones = jnp.ones((1, 128), BF16)
        lhs = jnp.concatenate([ones, a, b, c], 0)
        hit = jnp.where(columns == cell, 1.0, 0.0).astype(BF16)
        return total + dot(lhs, hit, NT)

    total = lax.fori_loop(0, 16, tally, jnp.zeros((4, N), F32))
    sums = total[1:2] + total[2:3] + total[3:4]
    for i in range(4):
        hist_s[i : i + 1, :] = total[0:1, 128 * i : 128 * i + 128]
        hist_s[4 + i : 5 + i, :] = sums[:, 128 * i : 128 * i + 128]
    weights = mix_v[...]
    weights = weights + (1.0 - jnp.sum(weights, 0, keepdims=True)) * (1.0 / MEMBERS)
    weights = weights.T
    w_high, w_rest = split(weights)
    w_left = weights - w_high.astype(F32)
    w_mid = w_left.astype(BF16)
    w_low = (w_left - w_mid.astype(F32)).astype(BF16)
    w_parts = jnp.concatenate([w_high, w_mid, w_low], 0)
    for copy in table_loads[2:]:
        copy.wait()

    scale = 2.0 * math.pi / N
    slot = lax.broadcasted_iota(jnp.int32, (16, QP), 1)
    slot = jnp.where(slot < KEEP, slot, jnp.where(slot < 2 * KEEP, slot - 2 * KEEP, 0))
    wave_x = slot.astype(F32) * scale
    wave_y = (lax.broadcasted_iota(jnp.int32, (16, QP), 0) + vs * W).astype(F32) * scale
    squared = wave_x * wave_x + wave_y * wave_y
    inverse = jnp.where(squared > 0, 1.0 / jnp.where(squared > 0, squared, 1.0), 0.0)

    def for_all(x):
        return jnp.concatenate([x] * 4, 0)

    finish(0, recv1.at[pl.ds(0, KEEP)])
    w = to_slots(gather_columns(recv1), tables[2][...], tables[3][...])
    spectrum[...] = w
    iw = times_i(w)
    pairs = [(wave_y * inverse, -wave_x * inverse), (wave_x, wave_y)]
    for h, pair in enumerate(pairs):
        lhs = jnp.concatenate(
            [jnp.concatenate([for_all(u) * iw, for_all(u) * -w], 1) for u in pair], 0
        )
        e = to_cells(lhs, tables[4][...], tables[5][...])
        parts = [stack_lanes(e[32 * g : 32 * g + 32]) for g in range(4)]
        for slot_ in range(4):
            got = pick_groups([turn(parts[g], g - slot_) for g in range(4)])
            for hi in range(4):
                for c in range(2):
                    send2[h, pl.ds(2 * W * (4 * hi + slot_) + W * c, W), :] = got[
                        32 * hi + 16 * c : 32 * hi + 16 * c + W
                    ]
        exchange(1 + h, rows_of(send2.at[h], 2 * W), rows_of(recv2.at[h], 2 * W), "space")

    def to_rows(h):
        high, low = split(recv2[h])
        out = dot(tables[6][...], jnp.concatenate([high, low], 1))
        return out[:, :128] + out[:, 128:] + dot(tables[7][...], high)

    finish(1, recv2.at[0])
    velocity = to_rows(0)
    finish(2, recv2.at[1])
    product = velocity * to_rows(1)
    product = product + pltpu.roll(product, 64, 1)
    first = lax.broadcasted_iota(jnp.int32, product.shape, 1) < 64
    rhs = jnp.concatenate([jnp.where(first, product, 0.0), jnp.where(first, 0.0, product)], 0)
    high, low = split(rhs)
    out = dot(tables[0][...], jnp.concatenate([high, low], 1))
    send3[...] = out[:, :128] + out[:, 128:] + dot(tables[1][...], high)
    exchange(3, rows_of(send3, W), rows_of(recv3, W), "space")

    @pl.when(fixed)
    def _():
        pltpu.make_async_copy(drive_in, drive, recv_sem.at[10]).start()

    @pl.when(moved)
    def _():
        copy_out(10, drive_in, drive, (vm, vs)).start()

    @pl.when(fixed)
    def _():
        pltpu.make_async_copy(hist_s, hist_r, recv_sem.at[11]).start()

    @pl.when(moved)
    def _():
        copy_out(11, hist_s, hist_r, (vm, vs)).start()

    finish(3, recv3.at[pl.ds(0, KEEP)])
    adv = to_slots(gather_columns(recv3), tables[2][...], tables[3][...])
    w = spectrum[...]
    new = w + DT_STEP * (-adv - VISCOSITY * for_all(squared) * w)
    e = to_cells(jnp.concatenate([new, times_i(new)], 1), tables[4][...], tables[5][...])
    parts = {
        c * 2 + k: stack_lanes(e[32 * k + 16 * c : 32 * k + 16 * c + 16])
        for k in range(2) for c in range(2)
    }
    for slot_ in range(4):
        got = pick_groups([turn(parts[g], g - slot_) for g in range(4)])
        for hi in range(4):
            send4[pl.ds(W * (4 * hi + slot_), W), :] = got[16 * hi : 16 * hi + W]
    exchange(4, rows_of(send4, W), rows_of(recv4, W), "space")

    finish(10, drive)
    finish(11, hist_r)
    forcing = DT_STEP * drive[...]
    counts = jnp.concatenate([hist_r[i : i + 1, :] for i in range(4)], 1)
    obs_sums = jnp.concatenate([hist_r[4 + i : 5 + i, :] for i in range(4)], 1)

    finish(4, recv4)
    modes = recv4[...].T
    high, low = split(modes)
    out = dot(jnp.concatenate([high[:64], low[:64]], 0), tables[8][...])
    out = out + dot(jnp.concatenate([high[64:], low[64:]], 0), tables[10][...])
    fresh = out[:64] + out[64:] + dot(high[:64], tables[9][...]) + dot(high[64:], tables[11][...])
    fresh = fresh + jnp.concatenate([forcing, forcing], 0)
    for k in range(2):
        for i in range(4):
            by_row[:, 4 * k + i, :] = fresh[32 * k : 32 * k + 32, 128 * i : 128 * i + 128]
    send5[...] = by_row[...].astype(BF16)
    exchange(5, lambda p: send5.at[p], lambda p: recv5.at[p], "member")

    finish(5, recv5)
    by_member[...] = recv5[...].astype(F32)
    for k in range(2):
        for i in range(4):
            members_v[i, pl.ds(k, 32, stride=2), :] = by_member[:, 4 * k + i, :]
    values = jnp.concatenate([members_v[i] for i in range(4)], 1)

    centre = jnp.sum(values, 0, keepdims=True) * (1.0 / MEMBERS)
    anomaly = values - centre
    innovation = obs_sums - counts * centre
    other = jnp.concatenate(
        [anomaly * counts, innovation, jnp.zeros((63, N), F32)], 0
    )
    a_high, a_low = split(anomaly)
    b_high, b_low = split(other)
    send_a[...] = dot(a_high, b_high, NT) + dot(a_high, b_low, NT) + dot(a_low, b_high, NT)
    exchange(7, rows_of(send_a, 4), rows_of(recv_a, 4), "space")

    mixed = dot(w_parts, values.astype(BF16))
    mixed = mixed[:64] + mixed[64:128] + mixed[128:]
    for i in range(4):
        mixed_v[i] = mixed[:, 128 * i : 128 * i + 128]
    for k in range(2):
        for i in range(4):
            send6[:, 4 * k + i, :] = mixed_v[i, pl.ds(k, 32, stride=2), :]
    finish(7, recv_a)
    chunk = recv_a[pl.ds(0, 4), :]
    for p in range(1, GS):
        chunk = chunk + recv_a[pl.ds(4 * p, 4), :]
    send_b[...] = chunk
    exchange(8, lambda p: send_b, rows_of(recv_b, 4), "member")

    scatter(
        6, BACK, back_peer, lambda d: (back_peer(d), vs), lambda p: send6.at[p], recv6.at[vm]
    )

    finish(8, recv_b)
    chunk = recv_b[pl.ds(0, 4), :]
    for p in range(1, GM):
        chunk = chunk + recv_b[pl.ds(4 * p, 4), :]
    send_c[...] = chunk
    exchange(9, lambda p: send_c, rows_of(recv_c, 4), "space")
    finish(6, recv6)
    stores = [
        pltpu.make_async_copy(
            recv6.at[:, 4 * k + i, :], rows_out.at[k, :, pl.ds(128 * i, 128)], store_sem.at[4 * k + i]
        )
        for k in range(2) for i in range(4)
    ]
    for copy in stores:
        copy.start()

    finish(9, recv_c)
    sums_out[...] = recv_c[...]

    for copy in stores:
        copy.wait()

    others = {
        0: send1.at[pl.ds(0, W * (GS - 1))],
        1: send2.at[0, pl.ds(0, 2 * W * (GS - 1))],
        2: send2.at[1, pl.ds(0, 2 * W * (GS - 1))],
        3: send3.at[pl.ds(0, W * (GS - 1))],
        4: send4.at[pl.ds(0, W * (GS - 1))],
        5: send5.at[pl.ds(0, GM - 1)],
        6: send6.at[pl.ds(0, GM - 1)],
        7: send_a.at[pl.ds(0, 4 * (GS - 1))],
        8: recv_b.at[pl.ds(0, 4 * (GM - 1))],
        9: recv_c.at[pl.ds(0, 4 * (GS - 1))],
    }

    def sent(k, ref):
        pltpu.make_async_copy(ref, ref, send_sem.at[k]).wait()

    for k, ref in others.items():
        sent(k, ref)

    @pl.when(moved)
    def _():
        sent(0, send1.at[pl.ds(0, W)])

    @pl.when(moved)
    def _():
        sent(6, send6.at[0])

    @pl.when(moved)
    def _():
        sent(10, drive_in)
        sent(11, hist_s)


def finish_kernel(rows, sums, analysis, spread, projection):
    analysis[...] = rows[...]
    full = sums[...]
    spread[...] = full[:, :64] * (1.0 / PROBES)
    shape = (64, 64)
    diagonal = lax.broadcasted_iota(jnp.int32, shape, 0) == lax.broadcasted_iota(jnp.int32, shape, 1)
    column = jnp.where(diagonal, full[:, 64:65], 0.0)
    projection[...] = jnp.sum(column, 0, keepdims=True) * (1.0 / math.sqrt(PROBES))


def on_device(swirls, driving, mixing, probes, observed):
    tables = [jnp.asarray(t) for t in make_tables()]
    vmem = pltpu.VMEM
    lanes = 128
    buffers = [
        (64, N), (ROWS, N), (ROWS, N), (64, 64),
    ]
    scratch = [vmem(shape, F32) for shape in buffers]
    scratch += [vmem((16, 128), jnp.int32), vmem((16, 128), F32)]
    for shape in TABLE_SHAPES:
        scratch += [vmem(shape, BF16)] * 2
    for shape in [
        (KEEP, lanes), (KEEP + 8, lanes),
        (2, 2 * KEEP, lanes), (2, 2 * KEEP, lanes),
        (KEEP, lanes), (KEEP + 8, lanes),
        (KEEP, lanes), (KEEP, lanes),
        (GM, 8, lanes, BF16), (GM, 8, lanes, BF16), (GM, 8, lanes), (GM, 8, lanes),
        (8, lanes), (8, lanes),
        (64, lanes), (64, lanes), (4, lanes), (4 * GM, lanes), (4, lanes), (64, lanes),
        (64, QP), (4, 64, lanes), (4, 64, lanes), (GM, 8, lanes), (GM, 8, lanes),
    ]:
        narrow = shape[-1] is BF16
        scratch.append(vmem(shape[:-1], BF16) if narrow else vmem(shape, F32))
    dma = pltpu.SemaphoreType.DMA
    scratch += [dma((5,)), dma((12,)), dma((12,)), dma((12,)), dma((8,))]
    anywhere = pl.BlockSpec(memory_space=pl.ANY)
    rows, sums = pl.pallas_call(
        kernel,
        out_shape=[
            jax.ShapeDtypeStruct((2, ROWS, N), F32),
            jax.ShapeDtypeStruct((64, lanes), F32),
        ],
        in_specs=[anywhere] * (5 + len(tables)),
        out_specs=[anywhere, pl.BlockSpec(memory_space=pltpu.VMEM)],
        scratch_shapes=scratch,
        compiler_params=pltpu.CompilerParams(
            collective_id=0, has_side_effects=True, vmem_limit_bytes=60 * 2**20
        ),
    )(
        swirls.reshape(64, N), driving, mixing, probes.reshape(16, 128), observed.reshape(16, 128),
        *tables,
    )
    analysis, spread, projection = pl.pallas_call(
        finish_kernel,
        out_shape=[
            jax.ShapeDtypeStruct((2, ROWS, N), F32),
            jax.ShapeDtypeStruct((64, 64), F32),
            jax.ShapeDtypeStruct((1, 64), F32),
        ],
        in_specs=[pl.BlockSpec(memory_space=pltpu.VMEM)] * 2,
        out_specs=[pl.BlockSpec(memory_space=pltpu.VMEM)] * 3,
        compiler_params=pltpu.CompilerParams(vmem_limit_bytes=60 * 2**20),
    )(rows, sums)
    return analysis, spread, projection.reshape(64)


def solution(mesh):
    return jax.shard_map(
        on_device,
        mesh=mesh,
        in_specs=(P("member", "space", None), P("space", None), P(), P("space"), P("space")),
        out_specs=(P("member", "space", None), P(), P()),
        check_vma=False,
    )
```

```python
import math

import jax
import jax.numpy as jnp
import ml_dtypes
import numpy as np
from jax import lax
from jax.experimental import pallas as pl
from jax.experimental.pallas import tpu as pltpu
from jax.sharding import PartitionSpec as P

N = 512
KEEP = 160
DT_STEP = 0.1
VISCOSITY = 0.05
MEMBERS = 64
ROWS = 32
PROBES = 32768
GM = 32
GS = 16
W = KEEP // GS
QP = 384

F32 = jnp.float32
BF16 = jnp.bfloat16
MESH = pl.DeviceIdType.MESH
NN = (((1,), (0,)), ((), ()))
NT = (((1,), (1,)), ((), ()))


def halves(table):
    high = table.astype(np.float32).astype(ml_dtypes.bfloat16)
    low = (table - high.astype(np.float64)).astype(np.float32).astype(ml_dtypes.bfloat16)
    return [high, low]


def make_tables():
    cells = np.arange(N)
    slots = np.arange(2 * KEEP)
    kx = np.where(slots < KEEP, slots, slots - 2 * KEEP)
    ky = np.arange(KEEP)

    def trig(a, b):
        angle = (a[:, None] * b[None, :] % N) * (2.0 * np.pi / N)
        return np.cos(angle), np.sin(angle)

    cos_y, sin_y = trig(ky, cells)
    rows_f = np.concatenate([cos_y, -sin_y], 1)
    cos_x, sin_x = trig(cells, kx)
    cols_f = np.zeros((2 * N, QP))
    cols_f[:N, : 2 * KEEP] = cos_x / (N * N)
    cols_f[N:, : 2 * KEEP] = sin_x / (N * N)
    cols_g = np.zeros((2 * QP, N))
    cols_g[: 2 * KEEP] = cos_x.T
    cols_g[QP : QP + 2 * KEEP] = sin_x.T
    count = np.where(ky == 0, 1.0, 2.0)[:, None]
    rows_g4 = np.stack([cos_y * count, -sin_y * count], 0)
    rows_g4 = rows_g4.reshape(2, GS, W, N).transpose(1, 0, 2, 3).reshape(2 * KEEP, N).T
    out = []
    for t in (rows_f, cols_f, cols_g, rows_g4, cos_y * count, -sin_y * count):
        out += halves(np.ascontiguousarray(t))
    return out


TABLE_SHAPES = [(KEEP, 2 * N), (2 * N, QP), (2 * QP, N), (N, 2 * KEEP), (KEEP, N), (KEEP, N)]


def dot(a, b, dims=NN):
    return lax.dot_general(a, b, dims, preferred_element_type=F32)


def split(x):
    high = x.astype(BF16)
    return high, (x - high.astype(F32)).astype(BF16)


def hops(step, ring):
    return min(step, ring - step)


NEAR = sorted(
    ((dx, a, b) for dx in range(4) for a in range(2) for b in range(2)),
    key=lambda d: (-hops(d[0], 4) - d[1], -d[2]),
)
FAR = sorted(
    ((dy, dz) for dy in range(8) for dz in range(4)),
    key=lambda d: (-hops(d[0], 8) - 2 * hops(d[1], 4), -d[0]),
)
BACK = sorted(
    ((dy, a, b) for dy in range(8) for a in range(2) for b in range(2)),
    key=lambda d: (-hops(d[0], 8), -d[1], -d[2]),
)


def lane_group(shape):
    return lax.div(lax.broadcasted_iota(jnp.int32, shape, len(shape) - 1), 32)


def pick_groups(pieces):
    group = lane_group(pieces[0].shape)
    low = jnp.where(group == 0, pieces[0], pieces[1])
    high = jnp.where(group == 2, pieces[2], pieces[3])
    return jnp.where(group < 2, low, high)


def turn(x, groups):
    groups %= 4
    return x if groups == 0 else pltpu.roll(x, 32 * groups, 1)


def gather_columns(recv):
    by_slot = [
        jnp.concatenate([recv[pl.ds(W * (4 * hi + slot), 16), :] for hi in range(4)], 0)
        for slot in range(4)
    ]
    rows = []
    for m in range(2):
        for c in range(2):
            t = c * 2 + m
            got = pick_groups([turn(by_slot[slot], slot - t) for slot in range(4)])
            rows.append(jnp.concatenate([got[16 * hi : 16 * hi + 16] for hi in range(4)], 1))
    return jnp.concatenate(rows, 0)


def times_i(w):
    return jnp.concatenate([-w[16:32], w[0:16], -w[48:64], w[32:48]], 0)


def to_slots(d, t_high, t_low):
    both = jnp.concatenate([d, -times_i(d)], 1)
    high, low = split(both)
    out = dot(jnp.concatenate([high, low], 0), t_high)
    return out[:64] + out[64:] + dot(high, t_low)


def to_cells(lhs, t_high, t_low):
    rows = lhs.shape[0]
    high, low = split(lhs)
    out = dot(jnp.concatenate([high, low], 0), t_high)
    return out[:rows] + out[rows:] + dot(high, t_low)


def stack_lanes(x):
    return jnp.concatenate([x[:, 128 * i : 128 * i + 128] for i in range(4)], 0)


def kernel(
    swirls, driving, mixing, probes, observed, *rest
):
    tables_hbm = rest[:12]
    rows_out, sums_out = rest[12:14]
    (
        f_v, drive_in, drive, mix_v, probes_v, obs_v,
        *more
    ) = rest[14:]
    tables = more[:12]
    (
        send1, recv1, send2, recv2, send3, recv3, send4, recv4, send5, recv5, send6, recv6,
        hist_s, hist_r, send_a, recv_a, send_b, recv_b, send_c, recv_c,
        spectrum, members_v, mixed_v, by_row, by_member,
        load_sem, table_sem, send_sem, recv_sem, store_sem,
    ) = more[12:]
    m, s = lax.axis_index("member"), lax.axis_index("space")
    x, z_hi = lax.div(s, 4), lax.rem(s, 4)
    z_lo, y, core = lax.div(m, 16), lax.rem(lax.div(m, 2), 8), lax.rem(m, 2)
    hi_hi, hi_lo = lax.div(z_hi, 2), lax.rem(z_hi, 2)
    pair = z_lo * 2 + core
    vm, vs = hi_hi * 16 + y * 2 + hi_lo, x * 4 + pair
    fixed = z_hi == pair
    moved = z_hi != pair
    xs = [x] + [lax.rem(x + d, 4) for d in range(1, 4)]
    ys = [y] + [lax.rem(y + d, 8) for d in range(1, 8)]
    zs = [z_hi] + [lax.rem(z_hi + d, 4) for d in range(1, 4)]
    lows, cores = [z_lo, 1 - z_lo], [core, 1 - core]
    near_m = {(a, b): lows[a] * 16 + y * 2 + cores[b] for a in range(2) for b in range(2)}
    back_m = [lows[0] * 16, lows[1] * 16]
    z_m = [lax.div(z, 2) * 16 + lax.rem(z, 2) for z in zs]

    def near_peer(d):
        return xs[d[0]] * 4 + lows[d[1]] * 2 + cores[d[2]]

    def near_device(d, z):
        return near_m[d[1], d[2]], xs[d[0]] * 4 + z

    def far_peer(d):
        return z_m[d[1]] + ys[d[0]] * 2

    def far_device(d, low, core_):
        return low * 16 + ys[d[0]] * 2 + core_, x * 4 + zs[d[1]]

    def back_peer(d):
        return back_m[d[1]] + ys[d[0]] * 2 + cores[d[2]]

    def there(target):
        return dict(device_id={"member": target[0], "space": target[1]}, device_id_type=MESH)

    barrier = pltpu.get_barrier_semaphore()

    def hello(target):
        pl.semaphore_signal(barrier, inc=1, **there(target))

    for d in FAR[:-1]:
        hello(far_device(d, z_lo, core))
        hello(far_device(d, hi_hi, hi_lo))
    for dx, dz in [(2, 2), (2, 1), (2, 3), (1, 2), (3, 2), (2, 0), (0, 2), (1, 1), (1, 3), (3, 1), (3, 3), (1, 0), (3, 0), (0, 1), (0, 3)]:
        hello((vm, xs[dx] * 4 + zs[dz]))
    for d in NEAR[:-1]:
        hello(near_device(d, z_hi))

    @pl.when(moved)
    def _():
        hello(far_device(FAR[-1], hi_hi, hi_lo))
        hello((vm, s))

    greeted = 2 * (GS + GM - 2) + 2 * moved.astype(jnp.int32)

    loads = [
        pltpu.make_async_copy(src, dst, load_sem.at[i])
        for i, (src, dst) in enumerate(
            [(swirls, f_v), (driving, drive_in), (mixing, mix_v), (probes, probes_v), (observed, obs_v)]
        )
    ]
    table_loads = [
        pltpu.make_async_copy(src, dst, table_sem.at[i])
        for i, (src, dst) in enumerate(zip(tables_hbm, tables))
    ]
    loads[0].start()
    for copy in table_loads[:2]:
        copy.start()
    for copy in loads[1:]:
        copy.start()
    for copy in table_loads[2:]:
        copy.start()

    def copy_out(k, src, dst, target):
        return pltpu.make_async_remote_copy(
            src_ref=src, dst_ref=dst, send_sem=send_sem.at[k], recv_sem=recv_sem.at[k], **there(target)
        )

    def exchange(k, src, dst, axis):
        me = vs if axis == "space" else vm
        for d in NEAR[:-1] if axis == "space" else FAR[:-1]:
            if axis == "space":
                p, target = near_peer(d), near_device(d, z_hi)
            else:
                p, target = far_peer(d), far_device(d, z_lo, core)
            copy_out(k, src(p), dst(me), target).start()
        pltpu.make_async_copy(src(me), dst(me), recv_sem.at[k]).start()

    def scatter(k, steps, peer, device, src, dst):
        for d in steps[:-1]:
            copy_out(k, src(peer(d)), dst, device(d)).start()
        p = peer(steps[-1])

        @pl.when(fixed)
        def _():
            pltpu.make_async_copy(src(p), dst, recv_sem.at[k]).start()

        @pl.when(moved)
        def _():
            copy_out(k, src(p), dst, device(steps[-1])).start()

    def finish(k, ref):
        pltpu.make_async_copy(ref, ref, recv_sem.at[k]).wait()

    def rows_of(ref, count):
        return lambda p: ref.at[pl.ds(count * p, count)]

    loads[0].wait()
    high, low = split(f_v[...])
    zero = jnp.zeros_like(high)

    def apart(x):
        return jnp.concatenate(
            [jnp.concatenate([x, zero], 1), jnp.concatenate([zero, x], 1)], 0
        )

    rhs_high = apart(high)
    table_loads[0].wait()
    table_loads[1].wait()
    out = dot(tables[0][...], jnp.concatenate([rhs_high, apart(low)], 0), NT)
    send1[...] = out[:, :128] + out[:, 128:] + dot(tables[1][...], rhs_high, NT)

    pl.semaphore_wait(barrier, greeted)
    scatter(
        0, NEAR, near_peer, lambda d: near_device(d, pair), rows_of(send1, W), recv1.at[pl.ds(W * s, W)]
    )

    for copy in loads[1:]:
        copy.wait()
    tail = pl.ds(KEEP, 8)
    recv1[tail, :] = jnp.zeros((8, 128), F32)
    recv3[tail, :] = jnp.zeros((8, 128), F32)
    columns = lax.broadcasted_iota(jnp.int32, (N, 128), 0) + m * N

    def tally(i, total):
        cell = probes_v[pl.ds(i, 1), :]
        obs = obs_v[pl.ds(i, 1), :]
        a, rest_ = split(obs)
        left = obs - a.astype(F32)
        b = left.astype(BF16)
        c = (left - b.astype(F32)).astype(BF16)
        ones = jnp.ones((1, 128), BF16)
        lhs = jnp.concatenate([ones, a, b, c], 0)
        hit = jnp.where(columns == cell, 1.0, 0.0).astype(BF16)
        return total + dot(lhs, hit, NT)

    total = lax.fori_loop(0, 16, tally, jnp.zeros((4, N), F32))
    sums = total[1:2] + total[2:3] + total[3:4]
    for i in range(4):
        hist_s[i : i + 1, :] = total[0:1, 128 * i : 128 * i + 128]
        hist_s[4 + i : 5 + i, :] = sums[:, 128 * i : 128 * i + 128]
    weights = mix_v[...]
    weights = weights + (1.0 - jnp.sum(weights, 0, keepdims=True)) * (1.0 / MEMBERS)
    weights = weights.T
    w_high, w_rest = split(weights)
    w_left = weights - w_high.astype(F32)
    w_mid = w_left.astype(BF16)
    w_low = (w_left - w_mid.astype(F32)).astype(BF16)
    w_parts = jnp.concatenate([w_high, w_mid, w_low], 0)
    for copy in table_loads[2:]:
        copy.wait()

    scale = 2.0 * math.pi / N
    slot = lax.broadcasted_iota(jnp.int32, (16, QP), 1)
    slot = jnp.where(slot < KEEP, slot, jnp.where(slot < 2 * KEEP, slot - 2 * KEEP, 0))
    wave_x = slot.astype(F32) * scale
    wave_y = (lax.broadcasted_iota(jnp.int32, (16, QP), 0) + vs * W).astype(F32) * scale
    squared = wave_x * wave_x + wave_y * wave_y
    inverse = jnp.where(squared > 0, 1.0 / jnp.where(squared > 0, squared, 1.0), 0.0)

    def for_all(x):
        return jnp.concatenate([x] * 4, 0)

    finish(0, recv1.at[pl.ds(0, KEEP)])
    w = to_slots(gather_columns(recv1), tables[2][...], tables[3][...])
    spectrum[...] = w
    iw = times_i(w)
    pairs = [(wave_y * inverse, -wave_x * inverse), (wave_x, wave_y)]
    for h, pair in enumerate(pairs):
        lhs = jnp.concatenate(
            [jnp.concatenate([for_all(u) * iw, for_all(u) * -w], 1) for u in pair], 0
        )
        e = to_cells(lhs, tables[4][...], tables[5][...])
        parts = [stack_lanes(e[32 * g : 32 * g + 32]) for g in range(4)]
        for slot_ in range(4):
            got = pick_groups([turn(parts[g], g - slot_) for g in range(4)])
            for hi in range(4):
                for c in range(2):
                    send2[h, pl.ds(2 * W * (4 * hi + slot_) + W * c, W), :] = got[
                        32 * hi + 16 * c : 32 * hi + 16 * c + W
                    ]
        exchange(1 + h, rows_of(send2.at[h], 2 * W), rows_of(recv2.at[h], 2 * W), "space")

    def to_rows(h):
        high, low = split(recv2[h])
        out = dot(tables[6][...], jnp.concatenate([high, low], 1))
        return out[:, :128] + out[:, 128:] + dot(tables[7][...], high)

    finish(1, recv2.at[0])
    velocity = to_rows(0)
    finish(2, recv2.at[1])
    product = velocity * to_rows(1)
    product = product + pltpu.roll(product, 64, 1)
    first = lax.broadcasted_iota(jnp.int32, product.shape, 1) < 64
    rhs = jnp.concatenate([jnp.where(first, product, 0.0), jnp.where(first, 0.0, product)], 0)
    high, low = split(rhs)
    out = dot(tables[0][...], jnp.concatenate([high, low], 1))
    send3[...] = out[:, :128] + out[:, 128:] + dot(tables[1][...], high)
    exchange(3, rows_of(send3, W), rows_of(recv3, W), "space")

    @pl.when(fixed)
    def _():
        pltpu.make_async_copy(drive_in, drive, recv_sem.at[10]).start()

    @pl.when(moved)
    def _():
        copy_out(10, drive_in, drive, (vm, vs)).start()

    @pl.when(fixed)
    def _():
        pltpu.make_async_copy(hist_s, hist_r, recv_sem.at[11]).start()

    @pl.when(moved)
    def _():
        copy_out(11, hist_s, hist_r, (vm, vs)).start()

    finish(3, recv3.at[pl.ds(0, KEEP)])
    adv = to_slots(gather_columns(recv3), tables[2][...], tables[3][...])
    w = spectrum[...]
    new = w + DT_STEP * (-adv - VISCOSITY * for_all(squared) * w)
    e = to_cells(jnp.concatenate([new, times_i(new)], 1), tables[4][...], tables[5][...])
    parts = {
        c * 2 + k: stack_lanes(e[32 * k + 16 * c : 32 * k + 16 * c + 16])
        for k in range(2) for c in range(2)
    }
    for slot_ in range(4):
        got = pick_groups([turn(parts[g], g - slot_) for g in range(4)])
        for hi in range(4):
            send4[pl.ds(W * (4 * hi + slot_), W), :] = got[16 * hi : 16 * hi + W]
    exchange(4, rows_of(send4, W), rows_of(recv4, W), "space")

    finish(10, drive)
    finish(11, hist_r)
    forcing = DT_STEP * drive[...]
    counts = jnp.concatenate([hist_r[i : i + 1, :] for i in range(4)], 1)
    obs_sums = jnp.concatenate([hist_r[4 + i : 5 + i, :] for i in range(4)], 1)

    finish(4, recv4)
    modes = recv4[...].T
    high, low = split(modes)
    out = dot(jnp.concatenate([high[:64], low[:64]], 0), tables[8][...])
    out = out + dot(jnp.concatenate([high[64:], low[64:]], 0), tables[10][...])
    fresh = out[:64] + out[64:] + dot(high[:64], tables[9][...]) + dot(high[64:], tables[11][...])
    fresh = fresh + jnp.concatenate([forcing, forcing], 0)
    for k in range(2):
        for i in range(4):
            by_row[:, 4 * k + i, :] = fresh[32 * k : 32 * k + 32, 128 * i : 128 * i + 128]
    send5[...] = by_row[...].astype(BF16)
    exchange(5, lambda p: send5.at[p], lambda p: recv5.at[p], "member")

    finish(5, recv5)
    by_member[...] = recv5[...].astype(F32)
    for k in range(2):
        for i in range(4):
            members_v[i, pl.ds(k, 32, stride=2), :] = by_member[:, 4 * k + i, :]
    values = jnp.concatenate([members_v[i] for i in range(4)], 1)

    centre = jnp.sum(values, 0, keepdims=True) * (1.0 / MEMBERS)
    anomaly = values - centre
    innovation = obs_sums - counts * centre
    other = jnp.concatenate(
        [anomaly * counts, innovation, jnp.zeros((63, N), F32)], 0
    )
    a_high, a_low = split(anomaly)
    b_high, b_low = split(other)
    send_a[...] = dot(a_high, b_high, NT) + dot(a_high, b_low, NT) + dot(a_low, b_high, NT)
    exchange(7, rows_of(send_a, 4), rows_of(recv_a, 4), "space")

    mixed = dot(w_parts, values.astype(BF16))
    mixed = mixed[:64] + mixed[64:128] + mixed[128:]
    for i in range(4):
        mixed_v[i] = mixed[:, 128 * i : 128 * i + 128]
    for k in range(2):
        for i in range(4):
            send6[:, 4 * k + i, :] = mixed_v[i, pl.ds(k, 32, stride=2), :]
    scatter(
        6, BACK, back_peer, lambda d: (back_peer(d), vs), lambda p: send6.at[p], recv6.at[vm]
    )

    finish(7, recv_a)
    chunk = recv_a[pl.ds(0, 4), :]
    for p in range(1, GS):
        chunk = chunk + recv_a[pl.ds(4 * p, 4), :]
    send_b[...] = chunk
    exchange(8, lambda p: send_b, rows_of(recv_b, 4), "member")

    finish(8, recv_b)
    chunk = recv_b[pl.ds(0, 4), :]
    for p in range(1, GM):
        chunk = chunk + recv_b[pl.ds(4 * p, 4), :]
    send_c[...] = chunk
    exchange(9, lambda p: send_c, rows_of(recv_c, 4), "space")
    finish(6, recv6)
    stores = [
        pltpu.make_async_copy(
            recv6.at[:, 4 * k + i, :], rows_out.at[k, :, pl.ds(128 * i, 128)], store_sem.at[4 * k + i]
        )
        for k in range(2) for i in range(4)
    ]
    for copy in stores:
        copy.start()

    finish(9, recv_c)
    sums_out[...] = recv_c[...]

    for copy in stores:
        copy.wait()

    others = {
        0: send1.at[pl.ds(0, W * (GS - 1))],
        1: send2.at[0, pl.ds(0, 2 * W * (GS - 1))],
        2: send2.at[1, pl.ds(0, 2 * W * (GS - 1))],
        3: send3.at[pl.ds(0, W * (GS - 1))],
        4: send4.at[pl.ds(0, W * (GS - 1))],
        5: send5.at[pl.ds(0, GM - 1)],
        6: send6.at[pl.ds(0, GM - 1)],
        7: send_a.at[pl.ds(0, 4 * (GS - 1))],
        8: recv_b.at[pl.ds(0, 4 * (GM - 1))],
        9: recv_c.at[pl.ds(0, 4 * (GS - 1))],
    }

    def sent(k, ref):
        pltpu.make_async_copy(ref, ref, send_sem.at[k]).wait()

    for k, ref in others.items():
        sent(k, ref)

    @pl.when(moved)
    def _():
        sent(0, send1.at[pl.ds(0, W)])

    @pl.when(moved)
    def _():
        sent(6, send6.at[0])

    @pl.when(moved)
    def _():
        sent(10, drive_in)
        sent(11, hist_s)


def finish_kernel(rows, sums, analysis, spread, projection):
    analysis[...] = rows[...]
    full = sums[...]
    spread[...] = full[:, :64] * (1.0 / PROBES)
    shape = (64, 64)
    diagonal = lax.broadcasted_iota(jnp.int32, shape, 0) == lax.broadcasted_iota(jnp.int32, shape, 1)
    column = jnp.where(diagonal, full[:, 64:65], 0.0)
    projection[...] = jnp.sum(column, 0, keepdims=True) * (1.0 / math.sqrt(PROBES))


def on_device(swirls, driving, mixing, probes, observed):
    tables = [jnp.asarray(t) for t in make_tables()]
    vmem = pltpu.VMEM
    lanes = 128
    buffers = [
        (64, N), (ROWS, N), (ROWS, N), (64, 64),
    ]
    scratch = [vmem(shape, F32) for shape in buffers]
    scratch += [vmem((16, 128), jnp.int32), vmem((16, 128), F32)]
    for shape in TABLE_SHAPES:
        scratch += [vmem(shape, BF16)] * 2
    for shape in [
        (KEEP, lanes), (KEEP + 8, lanes),
        (2, 2 * KEEP, lanes), (2, 2 * KEEP, lanes),
        (KEEP, lanes), (KEEP + 8, lanes),
        (KEEP, lanes), (KEEP, lanes),
        (GM, 8, lanes, BF16), (GM, 8, lanes, BF16), (GM, 8, lanes), (GM, 8, lanes),
        (8, lanes), (8, lanes),
        (64, lanes), (64, lanes), (4, lanes), (4 * GM, lanes), (4, lanes), (64, lanes),
        (64, QP), (4, 64, lanes), (4, 64, lanes), (GM, 8, lanes), (GM, 8, lanes),
    ]:
        narrow = shape[-1] is BF16
        scratch.append(vmem(shape[:-1], BF16) if narrow else vmem(shape, F32))
    dma = pltpu.SemaphoreType.DMA
    scratch += [dma((5,)), dma((12,)), dma((12,)), dma((12,)), dma((8,))]
    anywhere = pl.BlockSpec(memory_space=pl.ANY)
    rows, sums = pl.pallas_call(
        kernel,
        out_shape=[
            jax.ShapeDtypeStruct((2, ROWS, N), F32),
            jax.ShapeDtypeStruct((64, lanes), F32),
        ],
        in_specs=[anywhere] * (5 + len(tables)),
        out_specs=[anywhere, pl.BlockSpec(memory_space=pltpu.VMEM)],
        scratch_shapes=scratch,
        compiler_params=pltpu.CompilerParams(
            collective_id=0, has_side_effects=True, vmem_limit_bytes=60 * 2**20
        ),
    )(
        swirls.reshape(64, N), driving, mixing, probes.reshape(16, 128), observed.reshape(16, 128),
        *tables,
    )
    analysis, spread, projection = pl.pallas_call(
        finish_kernel,
        out_shape=[
            jax.ShapeDtypeStruct((2, ROWS, N), F32),
            jax.ShapeDtypeStruct((64, 64), F32),
            jax.ShapeDtypeStruct((1, 64), F32),
        ],
        in_specs=[pl.BlockSpec(memory_space=pltpu.VMEM)] * 2,
        out_specs=[pl.BlockSpec(memory_space=pltpu.VMEM)] * 3,
        compiler_params=pltpu.CompilerParams(vmem_limit_bytes=60 * 2**20),
    )(rows, sums)
    return analysis, spread, projection.reshape(64)


def solution(mesh):
    return jax.shard_map(
        on_device,
        mesh=mesh,
        in_specs=(P("member", "space", None), P("space", None), P(), P("space"), P("space")),
        out_specs=(P("member", "space", None), P(), P()),
        check_vma=False,
    )
```
